256 devices in a mesh: dp: 32 (over x_lo, z, core), expert: 8 (over x_hi, y).
Axes of the slice: x: 4 (x_hi: 2, x_lo: 2; x = x_hi * 2 + x_lo), y: 4, z: 8, core: 2. Of those that a mesh axis runs over, the one named last changes fastest.
Arguments:
- grad_out: bfloat16 [32768, 2560], P(('dp', 'expert')), may hold values from -6 to 6
- saved_input: bfloat16 [32768, 2560], P(('dp', 'expert')), may hold values from -6 to 6
- expert_ids: int32 [32768, 2], P(('dp', 'expert')), may hold values from 0 to 15, all different within a row; in each aligned block of 128 rows (0 to 127, 128 to 255, ...) at most 32 rows name the same one
- gate_weights: float32 [32768, 2], P(('dp', 'expert')), may hold values from 0.2 to 1
- up_weight: bfloat16 [16, 2560, 512], P('expert', 'dp'), may hold values from -0.125 to 0.125
- down_weight: bfloat16 [16, 512, 2560], P('expert', 'dp'), may hold values from -0.25 to 0.25
- engram_gate: float32 [32768, 4], P(('dp', 'expert')), may hold values from 0.1 to 1
- memory_owner: int32 [32768, 4], P(('dp', 'expert')), may hold values from 0 to 31, all different within a row; in each aligned block of 128 rows (0 to 127, 128 to 255, ...) at most 32 rows name the same one
- memory_slot: int32 [32768, 4], P(('dp', 'expert')), may hold values from 0 to 127
Outputs:
- grad_input: bfloat16 [32768, 2560], P(('dp', 'expert'))
- table_grad: float32 [4, 4096, 1280], P(None, ('dp', 'expert'))
The draws below stay inside these ranges and needn't reach their ends.
Inputs may be any that keep to these rules, and one draw needn't show every extreme that they name: `expert_ids`: each row names 2 different experts; among the rows of one device (aligned blocks of 128 rows) no expert is named more than 32 times, a bound that some block reaches. `memory_owner`: each row names 4 different owners; among the rows of one device (aligned blocks of 128 rows) no owner is named more than 32 times, a bound that some block reaches.
All inputs are finite; a program needn't handle non-finite values.
Results may differ from the reference program's by a relative error of at most 0.014.
Values may be sent and summed in bfloat16 or wider, within the bound.
A program may use at most 128 MiB of HBM per device.

```python
import math
import jax
import jax.numpy as jnp
import numpy as np
from jax import lax

D = 2560
HID = 512
TOP = 2
HEADS = 2
TOK_DEV = 128
SHARD = 128
EXPERTS = 16
TOKENS = 32768
ECAP = 32
LOOKUPS = 4
CAP = 32
TABLE_ROWS = 4096
N_DP = 32
N_EXPERT = 8


def plant(entries, rng, smallest, top_value):
    dims = entries.shape
    index_at = [jax.random.randint(jax.random.fold_in(rng, axis), (), 0, dims[axis]) for axis in range(len(dims))]
    entries = entries.at[tuple(index_at)].set(smallest)
    longest = dims.index(max(dims))
    index_at[longest] = (index_at[longest] + 1) % dims[longest]
    return entries.at[tuple(index_at)].set(top_value)


def shard_levels(own_key, dims, split, least, high):
    level = 1.0
    for axis_at, shards_of in split:
        draws = jax.random.uniform(jax.random.fold_in(jax.random.fold_in(own_key, 6), axis_at), (shards_of,), jnp.float32, least / len(split), high / len(split))
        level = level * jnp.repeat(jnp.exp(draws), dims[axis_at] // shards_of).reshape((-1,) + (1,) * (len(dims) - 1 - axis_at))
    return level


def rank_table(amount, skew):
    loads = [(1 << 20) // math.isqrt(standing ** skew) + 1 for standing in range(1, amount + 1)]
    scale = 1 + sum(loads) // (1 << 30)
    return np.cumsum(np.array([max(1, weight // scale) for weight in loads]))


def skewed_ids(stream_key, extent, count, skew):
    grid = rank_table(count, skew)
    lot = jax.random.randint(jax.random.fold_in(stream_key, 1), extent, 0, int(grid[count - 1]))
    grade = jnp.searchsorted(jnp.asarray(grid, jnp.int32), lot, side="right")
    return jax.random.permutation(jax.random.fold_in(stream_key, 2), count)[grade].astype(jnp.int32)


def assign_block(rng, own, number, rows, number_of, top, reach, skew):
    order = jax.random.permutation(rng, number_of)
    crowded, common = load_shares(number_of, rows * top, reach, skew, True), load_shares(number_of, rows * top, reach, skew, False)
    places = jnp.arange(number_of)

    def named(tallies, rotation):
        used = int((tallies > 0).sum())
        fixed = max(1, used // 4)
        passed = fixed + (places - fixed + rotation * (used - fixed)) % max(1, number_of - fixed)
        return jnp.zeros((number_of,), jnp.int32).at[order[jnp.where(places < fixed, places, passed)]].set(jnp.asarray(tallies, jnp.int32))

    tallies = jnp.where(number % 4 == 0, named(crowded, number // 4), named(common, number - number // 4 - 1))
    mixed = jax.random.permutation(jax.random.fold_in(own, 3), number_of)
    giver, receiver = mixed[0:number_of // 2 * 2:2], mixed[1:number_of // 2 * 2:2]
    margin = jnp.minimum(tallies[giver] - 1, reach - tallies[receiver]) // 2
    margin = jnp.where((giver == order[0]) | (receiver == order[0]) | (tallies[receiver] == 0), 0, jnp.maximum(margin, 0))
    passed = jax.random.randint(jax.random.fold_in(own, 4), (number_of // 2,), 0, 1 << 20) % (margin + 1)
    tallies = tallies.at[giver].add(-passed).at[receiver].add(passed)
    labels = jnp.searchsorted(jnp.cumsum(tallies), jnp.arange(rows * top), side="right").astype(jnp.int32)
    grid = labels.reshape(top, rows).T
    grid = grid[jax.random.permutation(jax.random.fold_in(own, 1), rows)]
    rotation = jax.random.randint(jax.random.fold_in(own, 2), (rows, 1), 0, top)
    return jnp.take_along_axis(grid, (jnp.arange(top)[None, :] + rotation) % top, axis=1)


def load_shares(number_of, total, limit, skew, full):
    weights = [(1 << 20) // math.isqrt(grade ** skew) + 1 for grade in range(1, number_of + 1)]
    largest = limit if full else min(limit, max(-(-total // number_of), total * weights[0] // sum(weights)))
    least = 1 if total - largest >= number_of - 1 else 0
    given, surplus = [largest] + [least] * (number_of - 1), total - largest - least * (number_of - 1)
    while surplus > 0:
        candidates = [i for i in range(1, number_of) if given[i] < largest] or [i for i in range(1, number_of) if given[i] < limit]
        pool, budget = sum([weights[i] for i in candidates]), surplus
        for i in candidates:
            addition = min(limit - given[i], max(1, budget * weights[i] // pool), surplus)
            given[i] = given[i] + addition
            surplus = surplus - addition
    return np.array(given)


def scatter_about(stream_key, dims, deviation, limit, shards=(), kind=jnp.bfloat16):
    drawn = deviation * jax.random.normal(stream_key, dims, jnp.float32)
    if shards:
        drawn = drawn * shard_levels(stream_key, dims, shards, -0.22, 0.18)
    return jnp.clip(drawn, -limit, limit).astype(kind)


def setup_inputs(seed: int = 0) -> dict:
    key_of = jax.random.split(jax.random.key(seed), 10)
    grad_out = scatter_about(key_of[0], (TOKENS, D), 1.0, 6.0, ((0, 256),))
    saved_input = scatter_about(key_of[1], (TOKENS, D), 1.0, 6.0, ((0, 256),))
    expert_ids_keys = jax.random.split(jax.random.fold_in(key_of[2], 1), TOKENS // TOK_DEV)
    expert_ids_turns = jax.random.permutation(jax.random.fold_in(key_of[2], 3), TOKENS // TOK_DEV)
    expert_ids = jax.vmap(lambda own, number: assign_block(jax.random.fold_in(key_of[2], 2), own, number, TOK_DEV, EXPERTS, TOP, ECAP, 2))(expert_ids_keys, expert_ids_turns).reshape((TOKENS, TOP))
    gate_weights = jnp.clip(0.2 + 0.8 * jax.random.uniform(key_of[3], (TOKENS, TOP), jnp.float32) ** shard_levels(key_of[3], (TOKENS, TOP), ((0, 256),), -0.2, 0.2), 0.2, 1.0)
    up_weight = scatter_about(key_of[4], (EXPERTS, D, HID), D ** -0.5, 0.125, ((0, 8), (1, 32)))
    down_weight = scatter_about(key_of[5], (EXPERTS, HID, D), HID ** -0.5, 0.25, ((0, 8), (1, 32)))
    engram_gate = jnp.clip(0.1 + 0.9 * jax.random.uniform(key_of[6], (TOKENS, LOOKUPS), jnp.float32) ** shard_levels(key_of[6], (TOKENS, LOOKUPS), ((0, 256),), -0.2, 0.2), 0.1, 1.0)
    memory_owner_keys = jax.random.split(jax.random.fold_in(key_of[7], 1), TOKENS // TOK_DEV)
    memory_owner_turns = jax.random.permutation(jax.random.fold_in(key_of[7], 3), TOKENS // TOK_DEV)
    memory_owner = jax.vmap(lambda own, number: assign_block(jax.random.fold_in(key_of[7], 2), own, number, TOK_DEV, N_DP, LOOKUPS, CAP, 2))(memory_owner_keys, memory_owner_turns).reshape((TOKENS, LOOKUPS))
    memory_slot = plant(skewed_ids(key_of[8], (TOKENS, LOOKUPS), SHARD, 2), jax.random.fold_in(key_of[8], 3), 0, SHARD - 1).astype(jnp.int32)
    return {"grad_out": grad_out, "saved_input": saved_input, "expert_ids": expert_ids, "gate_weights": gate_weights, "up_weight": up_weight, "down_weight": down_weight, "engram_gate": engram_gate, "memory_owner": memory_owner, "memory_slot": memory_slot}


def silu_slope(pre):
    sig = jax.nn.sigmoid(pre)
    return sig * (1.0 + pre * (1.0 - sig))


def reference(grad_out, saved_input, expert_ids, gate_weights, up_weight, down_weight, engram_gate, memory_owner, memory_slot):
    tokens = grad_out.shape[0]
    most = N_DP * N_EXPERT * ECAP

    def per_expert(total, expert):
        hits = expert_ids == expert
        chosen = jnp.any(hits, axis=1)
        weight = jnp.sum(jnp.where(hits, gate_weights, jnp.zeros_like(gate_weights)), axis=1)
        index = jnp.nonzero(chosen, size=most, fill_value=0)[0].astype(jnp.int32)
        valid = jnp.arange(most, dtype=jnp.int32) < jnp.sum(chosen.astype(jnp.int32))
        inputs = saved_input[index]
        grads = grad_out[index]
        up_one = lax.dynamic_index_in_dim(up_weight, expert, 0, keepdims=False)
        down_one = lax.dynamic_index_in_dim(down_weight, expert, 0, keepdims=False)
        pre = jnp.dot(inputs, up_one, preferred_element_type=jnp.float32)
        back = jnp.dot(grads, down_one.T, preferred_element_type=jnp.float32)
        slope = (back * silu_slope(pre)).astype(jnp.bfloat16)
        expert_grad = jnp.dot(slope, up_one.T, preferred_element_type=jnp.float32).astype(jnp.bfloat16)
        term = jnp.where(valid[:, None], weight[index][:, None] * expert_grad.astype(jnp.float32), 0.0)
        return total.at[index].add(term), None

    total, unused = lax.scan(per_expert, jnp.zeros((tokens, D), jnp.float32), jnp.arange(EXPERTS, dtype=jnp.int32))
    width = D // 2
    halves = grad_out.reshape(tokens, 2, width)
    rows = (engram_gate[:, :, None] * jnp.repeat(halves, HEADS, axis=1).astype(jnp.float32)).astype(jnp.bfloat16)
    target = (jnp.arange(LOOKUPS, dtype=jnp.int32)[None, :] * TABLE_ROWS + memory_owner * SHARD + memory_slot).reshape(-1)
    table = jnp.zeros((LOOKUPS * TABLE_ROWS, width), jnp.float32).at[target].add(rows.reshape(-1, width).astype(jnp.float32))
    return total.astype(jnp.bfloat16), table.reshape(LOOKUPS, TABLE_ROWS, width)
```

```python
import functools

import jax
import jax.numpy as jnp
from jax import lax
from jax.experimental import pallas as pl
from jax.experimental.pallas import tpu as pltpu
from jax.sharding import PartitionSpec as P

MESH = pl.DeviceIdType.MESH
F32 = jnp.float32
BF16 = jnp.bfloat16
NZ = 8
XL = 2
CORES = 2
NE = 8
EXPERTS = NE * CORES
TOK = 128
D = 2560
HID = 512
CAP = 32
HALF = D // 2
Q = 2
QW = HALF // Q
UPR = D // (XL * NZ * CORES)
DNR = HID // (XL * NZ * CORES)
BLOCKS = NZ * CORES
GROUP = XL * CORES * NE
TROWS = GROUP * 2 * 16


def mod(value, size):
    return lax.rem(value + size, size)


def nt_dot(a, b):
    return lax.dot_general(a, b, (((1,), (1,)), ((), ())), preferred_element_type=F32)


def kernel(
    grad_ref, input_ref, up_ref, down_ref, emeta_ref, mmeta_ref,
    gi_ref, table_ref,
    up_buf, down_buf, pick, blend, send_x, send_g, got_x, got_g, slope_buf, ret_send, ret_got,
    gbuf, mbuf, sel, dense, rs_got,
    pre_recv, pre_send, w_recv, w_send, m_recv, m_send, t_recv, t_send,
    d_recv, d_send, r_recv, r_send, rs_recv, rs_send,
):
    dp = lax.axis_index("dp")
    e = lax.axis_index("expert")
    c = lax.rem(dp, 2)
    z = lax.rem(dp // 2, NZ)
    xl = dp // (2 * NZ)
    oc = 1 - c
    oxl = 1 - xl

    def dp_of(xl_, z_, c_):
        return (xl_ * NZ + z_) * 2 + c_

    def dev(xl_, z_, c_, e_):
        return {"dp": dp_of(xl_, z_, c_), "expert": e_}

    sibling = dev(xl, z, oc, e)
    ring = (dev(xl, mod(z + 1, NZ), c, e), dev(xl, mod(z - 1, NZ), c, e))
    me16 = e * 2 + c
    me32 = (xl * 2 + c) * NE + e

    def peer16(m):
        return dev(xl, z, lax.rem(m, 2), m // 2)

    def peer32(m):
        return dev(m // (2 * NE), z, lax.rem(m // NE, 2), lax.rem(m, NE))

    def remote(src, dst, send, recv, device):
        return pltpu.make_async_remote_copy(
            src_ref=src, dst_ref=dst, send_sem=send, recv_sem=recv,
            device_id=device, device_id_type=MESH,
        )

    barrier = pltpu.get_barrier_semaphore()
    for d in range(2):
        pl.semaphore_signal(barrier, inc=1, device_id=ring[d], device_id_type=MESH)

    @pl.loop(1, GROUP)
    def _(k):
        pl.semaphore_signal(
            barrier, inc=1, device_id=peer32(lax.rem(me32 + k, GROUP)), device_id_type=MESH
        )

    def up_rows(dp_, count):
        return pl.ds(pl.multiple_of(dp_ * UPR, 16), count)

    def down_rows(dp_, count):
        return pl.ds(pl.multiple_of(dp_ * DNR, 16), count)

    def tok_rows(block):
        return pl.ds(pl.multiple_of(block * TOK, TOK), TOK)

    def half_cols(order, q):
        return pl.ds(pl.multiple_of(order * HALF + q * QW, 128), QW)

    up_buf[up_rows(dp, UPR), :] = up_ref[c]
    down_buf[down_rows(dp, DNR), :] = down_ref[c]
    mine = z * 2 + c
    mbuf[mine] = mmeta_ref[c]
    for q in range(Q):
        gbuf[q, tok_rows(mine), :] = grad_ref[:, half_cols(c, q)]

    pl.semaphore_wait(barrier, GROUP - 1 + 2)

    pre = []
    for at, (src_core, device) in enumerate(
        ((oc, sibling), (c, dev(oxl, z, c, e)), (oc, dev(oxl, z, oc, e)))
    ):
        pre.append(remote(
            up_ref.at[src_core], up_buf.at[up_rows(dp, UPR)],
            pre_send.at[2 * at], pre_recv.at[2 * at], device,
        ))
        pre.append(remote(
            down_ref.at[src_core], down_buf.at[down_rows(dp, DNR)],
            pre_send.at[2 * at + 1], pre_recv.at[2 * at + 1], device,
        ))
    pre.append(remote(mmeta_ref.at[oc], mbuf.at[mine], pre_send.at[6], pre_recv.at[6], sibling))
    for q in range(Q):
        pre.append(remote(
            grad_ref.at[:, half_cols(oc, q)], gbuf.at[q, tok_rows(mine)],
            pre_send.at[7 + q], pre_recv.at[7 + q], sibling,
        ))
    for copy in pre:
        copy.start()
    theirs = z * 2 + oc
    arrivals = []
    for dp_ in (dp_of(xl, z, oc), dp_of(oxl, z, c), dp_of(oxl, z, oc)):
        arrivals.append(up_buf.at[up_rows(dp_, UPR)])
        arrivals.append(down_buf.at[down_rows(dp_, DNR)])
    arrivals.append(mbuf.at[theirs])
    for q in range(Q):
        arrivals.append(gbuf.at[q, tok_rows(theirs)])

    def pre_wait(at):
        remote(arrivals[at], arrivals[at], pre_send.at[at], pre_recv.at[at], sibling).wait_recv()

    def origin(d, s):
        return mod(z - s, NZ) if d == 0 else mod(z + s, NZ)

    def ring_block(kind, d, zs):
        if kind == "up":
            return up_buf.at[up_rows(dp_of((xl, oxl)[d], zs, 0), 2 * UPR)]
        if kind == "down":
            return down_buf.at[down_rows(dp_of((xl, oxl)[d], zs, 0), 2 * DNR)]
        block = zs * 2 + (c, oc)[d]
        if kind == "meta":
            return mbuf.at[block]
        return gbuf.at[kind, tok_rows(block)]

    def ring_sems(kind, d, s):
        if kind == "up":
            return w_send.at[0], w_recv.at[d, 0, s]
        if kind == "down":
            return w_send.at[1], w_recv.at[d, 1, s]
        if kind == "meta":
            return m_send, m_recv.at[d, s]
        return t_send.at[kind], t_recv.at[d, kind, s]

    def ring_send(kind, d, s):
        block = ring_block(kind, d, origin(d, s))
        send, recv = ring_sems(kind, d, s)
        remote(block, block, send, recv, ring[d]).start()

    def ring_wait(kind, d, s):
        block = ring_block(kind, d, origin(d, s + 1))
        send, recv = ring_sems(kind, d, s)
        remote(block, block, send, recv, ring[d]).wait_recv()

    def ring_step(kinds, s):
        for kind in kinds:
            for d in range(2):
                ring_wait(kind, d, s - 1)
                if s < NZ - 1:
                    ring_send(kind, d, s)

    ids = (emeta_ref[0:1, :], emeta_ref[1:2, :])
    gates = (emeta_ref[2:3, :], emeta_ref[3:4, :])
    numbers = lax.broadcasted_iota(jnp.int32, (EXPERTS, TOK), 0).astype(F32)
    zeros = jnp.zeros((EXPERTS, TOK), F32)
    hit0, hit1 = numbers == ids[0], numbers == ids[1]
    hits = jnp.where(hit0 | hit1, 1.0, 0.0)
    weight = jnp.where(hit0, gates[0], zeros) + jnp.where(hit1, gates[1], zeros)
    earlier = jnp.where(
        lax.broadcasted_iota(jnp.int32, (TOK, TOK), 0)
        < lax.broadcasted_iota(jnp.int32, (TOK, TOK), 1),
        1.0, 0.0,
    ).astype(BF16)
    rank = jnp.dot(hits.astype(BF16), earlier, preferred_element_type=F32)
    place = jnp.where(hits > 0.5, rank, -1.0)
    slots = lax.broadcasted_iota(jnp.int32, (CAP, TOK), 0).astype(F32)
    for x in range(EXPERTS):
        chosen = slots == place[x : x + 1, :]
        pick[x * CAP : (x + 1) * CAP, :] = jnp.where(chosen, 1.0, 0.0).astype(BF16)
        blend[x * CAP : (x + 1) * CAP, :] = jnp.where(chosen, weight[x : x + 1, :], 0.0)

    pre_wait(0)
    ring_send("up", 0, 0)
    pre_wait(1)
    ring_send("down", 0, 0)
    pre_wait(6)
    for d in range(2):
        ring_send("meta", d, 0)

    own = me16 // 4

    def dispatch(i):
        first = lax.rem(own + i, 4) * 4
        rows = pl.ds(pl.multiple_of(first * CAP, 128), 4 * CAP)
        onehot = pick[rows, :]

        @pl.loop(0, 5)
        def _(n):
            cols = pl.ds(pl.multiple_of(n * 512, 512), 512)
            send_x[rows, cols] = jnp.dot(
                onehot, input_ref[:, cols], preferred_element_type=F32
            ).astype(BF16)
            send_g[rows, cols] = jnp.dot(
                onehot, grad_ref[:, cols], preferred_element_type=F32
            ).astype(BF16)

    def slot_rows(m):
        return pl.ds(pl.multiple_of(m * CAP, CAP), CAP)

    def dispatch_sends(i):
        @pl.loop(0, 4)
        def _(k):
            m = lax.rem(own + i, 4) * 4 + lax.rem(me16 + k, 4)

            @pl.when(m != me16)
            def _():
                remote(
                    send_x.at[slot_rows(m)], got_x.at[slot_rows(me16)],
                    d_send.at[0], d_recv.at[0], peer16(m),
                ).start()
                remote(
                    send_g.at[slot_rows(m)], got_g.at[slot_rows(me16)],
                    d_send.at[1], d_recv.at[1], peer16(m),
                ).start()

    dispatch(1)
    dispatch_sends(1)
    pre_wait(2)
    pre_wait(4)
    ring_send("up", 1, 0)
    pre_wait(3)
    pre_wait(5)
    ring_send("down", 1, 0)
    for i in (2, 3, 0):
        dispatch(i)
        dispatch_sends(i)
    got_x[slot_rows(me16), :] = send_x[slot_rows(me16), :]
    got_g[slot_rows(me16), :] = send_g[slot_rows(me16), :]

    for s in range(1, 4):
        ring_step(("up", "down", "meta"), s)
    pre_wait(7)
    for s in range(4, 8):
        ring_step(("up", "down", "meta"), s)
        if s == 4:
            for d in range(2):
                ring_send(0, d, 0)
        else:
            ring_step((0,), s - 4)

    def all_bytes(ref, sem):
        pltpu.make_async_copy(ref, ref, sem).wait()

    some = pl.ds(0, (EXPERTS - 1) * CAP)
    all_bytes(got_x.at[some], d_recv.at[0])
    all_bytes(got_g.at[some], d_recv.at[1])

    def expert(i):
        rows = pl.ds(i * 256, 256)

        @pl.loop(0, 2)
        def _(n):
            cols = pl.ds(pl.multiple_of(n * 256, 256), 256)
            before = jnp.dot(got_x[rows, :], up_buf[:, cols], preferred_element_type=F32)
            back = nt_dot(got_g[rows, :], down_buf[cols, :])
            sig = 1.0 / (1.0 + jnp.exp(-before))
            slope_buf[:, cols] = (back * sig * (1.0 + before * (1.0 - sig))).astype(BF16)

        @pl.loop(0, D // 256)
        def _(n):
            cols = pl.ds(pl.multiple_of(n * 256, 256), 256)
            ret_send[rows, cols] = nt_dot(slope_buf[...], up_buf[cols, :]).astype(BF16)

        @pl.loop(0, 8)
        def _(k):
            m = i * 8 + lax.rem(me16 + k, 8)

            @pl.when(m != me16)
            def _():
                remote(
                    ret_send.at[slot_rows(m)], ret_got.at[slot_rows(me16)],
                    r_send, r_recv, peer16(m),
                ).start()

    pre_wait(8)
    expert(0)
    ring_step((0,), 4)
    for d in range(2):
        ring_send(1, d, 0)
    expert(1)
    ret_got[slot_rows(me16), :] = ret_send[slot_rows(me16), :]
    ring_step((0, ), 5)
    ring_step((1, ), 1)

    targets = (lax.broadcasted_iota(jnp.int32, (TROWS, TOK), 0) + z * TROWS).astype(F32)

    def select(block):
        cols = pl.ds(pl.multiple_of(block * TOK, TOK), TOK)
        meta = mbuf[block]
        one = jnp.where(targets == meta[1:2, :], meta[3:4, :], 0.0)
        sel[:, cols] = jnp.where(targets == meta[0:1, :], meta[2:3, :], one).astype(BF16)

    pl.loop(0, BLOCKS // 2)(select)
    ring_step((0, ), 6)
    ring_step((1, ), 2)
    pl.loop(BLOCKS // 2, BLOCKS)(select)
    ring_step((0, ), 7)
    ring_step((1, ), 3)

    def table_rows(m):
        return pl.ds(pl.multiple_of(m * 32, 32), 32)

    def table_part(q):
        @pl.loop(0, TROWS // 256)
        def _(i):
            rows = pl.ds(pl.multiple_of(i * 256, 256), 256)
            dense[q, rows, :] = jnp.dot(
                sel[rows, :], gbuf[q], preferred_element_type=F32
            ).astype(BF16)

        @pl.loop(1, GROUP)
        def _(k):
            m = lax.rem(me32 + k, GROUP)
            remote(
                dense.at[q, table_rows(m)], rs_got.at[q, (c * 2 + xl) * NE + e],
                rs_send.at[q], rs_recv.at[q], peer32(m),
            ).start()

        rs_got[q, (c * 2 + xl) * NE + e] = dense[q, table_rows(me32), :]

    def table_sum(q):
        all_bytes(rs_got.at[q, pl.ds(0, GROUP - 1)], rs_recv.at[q])
        for order in range(2):
            total = rs_got[q, order * 16].astype(F32)
            for k in range(1, 16):
                total += rs_got[q, order * 16 + k].astype(F32)
            table_ref[order * 2 : order * 2 + 2, :, q * QW : (q + 1) * QW] = total.reshape(
                2, 16, QW
            )

    table_part(0)
    for s in range(4, 7):
        ring_step((1, ), s)

    all_bytes(ret_got.at[some], r_recv)
    mix = blend[...].T.astype(BF16)

    @pl.loop(0, D // 256)
    def _(n):
        cols = pl.ds(pl.multiple_of(n * 256, 256), 256)
        gi_ref[:, cols] = jnp.dot(mix, ret_got[:, cols], preferred_element_type=F32).astype(BF16)

    ring_step((1, ), 7)
    table_part(1)
    table_sum(0)
    table_sum(1)

    for copy in pre:
        copy.wait_send()
    sends = 2 * (NZ - 1)
    all_bytes(up_buf.at[pl.ds(0, sends * 2 * UPR)], w_send.at[0])
    all_bytes(down_buf.at[pl.ds(0, sends * 2 * DNR)], w_send.at[1])
    all_bytes(mbuf.at[pl.ds(0, sends)], m_send)
    for q in range(Q):
        all_bytes(gbuf.at[q, pl.ds(0, sends * TOK)], t_send.at[q])
        all_bytes(dense.at[q, pl.ds(0, (GROUP - 1) * 32)], rs_send.at[q])
    all_bytes(send_x.at[some], d_send.at[0])
    all_bytes(send_g.at[some], d_send.at[1])
    all_bytes(ret_send.at[some], r_send)


def per_device(
    grad_out, saved_input, expert_ids, gate_weights, up_weight, down_weight,
    engram_gate, memory_owner, memory_slot,
):
    emeta = jnp.concatenate(
        [expert_ids.astype(F32).T, gate_weights.T, jnp.zeros((4, TOK), F32)], axis=0
    )
    head = jnp.arange(4, dtype=jnp.int32)[None, :] % 2
    core = memory_owner % 2
    zs = (memory_owner // 2) % NZ
    xs = memory_owner // (2 * NZ)
    row = (((zs * XL + xs) * 2 + core) * NE + memory_slot // 16) * 32
    row = row + head * 16 + memory_slot % 16
    rows_t = row.astype(F32).T.reshape(2, 2, TOK)
    gates_t = engram_gate.T.reshape(2, 2, TOK)
    mmeta = jnp.concatenate([rows_t, gates_t, jnp.zeros((2, 4, TOK), F32)], axis=1)

    vmem = pl.BlockSpec(memory_space=pltpu.VMEM)
    dma = pltpu.SemaphoreType.DMA
    return pl.pallas_call(
        kernel,
        out_shape=(
            jax.ShapeDtypeStruct((TOK, D), BF16),
            jax.ShapeDtypeStruct((4, 16, HALF), F32),
        ),
        in_specs=[vmem] * 6,
        out_specs=(vmem, vmem),
        scratch_shapes=[
            pltpu.VMEM((D, HID), BF16),
            pltpu.VMEM((HID, D), BF16),
            pltpu.VMEM((EXPERTS * CAP, TOK), BF16),
            pltpu.VMEM((EXPERTS * CAP, TOK), F32),
            pltpu.VMEM((EXPERTS * CAP, D), BF16),
            pltpu.VMEM((EXPERTS * CAP, D), BF16),
            pltpu.VMEM((EXPERTS * CAP, D), BF16),
            pltpu.VMEM((EXPERTS * CAP, D), BF16),
            pltpu.VMEM((256, HID), BF16),
            pltpu.VMEM((EXPERTS * CAP, D), BF16),
            pltpu.VMEM((EXPERTS * CAP, D), BF16),
            pltpu.VMEM((Q, BLOCKS * TOK, QW), BF16),
            pltpu.VMEM((BLOCKS, 8, TOK), F32),
            pltpu.VMEM((TROWS, BLOCKS * TOK), BF16),
            pltpu.VMEM((Q, TROWS, QW), BF16),
            pltpu.VMEM((Q, GROUP, 32, QW), BF16),
            dma((7 + Q,)),
            dma((7 + Q,)),
            dma((2, 2, NZ - 1)),
            dma((2,)),
            dma((2, NZ - 1)),
            dma(()),
            dma((2, Q, NZ - 1)),
            dma((Q,)),
            dma((2,)),
            dma((2,)),
            dma(()),
            dma(()),
            dma((Q,)),
            dma((Q,)),
        ],
        compiler_params=pltpu.CompilerParams(
            collective_id=0, has_side_effects=True, vmem_limit_bytes=58 * 1024 * 1024
        ),
        cost_estimate=pl.CostEstimate(
            flops=10_000_000_000, bytes_accessed=4_000_000, transcendentals=262_144
        ),
    )(grad_out, saved_input, up_weight, down_weight, emeta, mmeta)


def solution(mesh):
    tokens = P(("dp", "expert"), None)
    return jax.shard_map(
        per_device,
        mesh=mesh,
        in_specs=(
            tokens, tokens, tokens, tokens,
            P("expert", "dp", None), P("expert", "dp", None),
            tokens, tokens, tokens,
        ),
        out_specs=(tokens, P(None, ("dp", "expert"), None)),
        check_vma=False,
    )
```

```python
import functools

import jax
import jax.numpy as jnp
from jax import lax
from jax.experimental import pallas as pl
from jax.experimental.pallas import tpu as pltpu
from jax.sharding import PartitionSpec as P

MESH = pl.DeviceIdType.MESH
F32 = jnp.float32
BF16 = jnp.bfloat16
NZ = 8
XL = 2
CORES = 2
NE = 8
EXPERTS = NE * CORES
TOK = 128
D = 2560
HID = 512
CAP = 32
HALF = D // 2
Q = 5
QW = HALF // Q
UPR = D // (XL * NZ * CORES)
DNR = HID // (XL * NZ * CORES)
BLOCKS = NZ * CORES
GROUP = XL * CORES * NE
TROWS = GROUP * 2 * 16


def mod(value, size):
    return lax.rem(value + size, size)


def nt_dot(a, b):
    return lax.dot_general(a, b, (((1,), (1,)), ((), ())), preferred_element_type=F32)


def kernel(
    grad_ref, input_ref, up_ref, down_ref, emeta_ref, mmeta_ref,
    gi_ref, table_ref,
    up_buf, down_buf, pick, blend, send_x, send_g, got_x, got_g, slope_buf, ret_send, ret_got,
    gbuf, mbuf, sel, dense, rs_got,
    pre_recv, pre_send, w_recv, w_send, x_recv, x_send, m_recv, m_send, t_recv, t_send,
    d_recv, d_send, r_recv, r_send, rs_recv, rs_send,
):
    dp = lax.axis_index("dp")
    e = lax.axis_index("expert")
    c = lax.rem(dp, 2)
    z = lax.rem(dp // 2, NZ)
    xl = dp // (2 * NZ)
    oc = 1 - c
    oxl = 1 - xl

    def dp_of(xl_, z_, c_):
        return (xl_ * NZ + z_) * 2 + c_

    def dev(xl_, z_, c_, e_):
        return {"dp": dp_of(xl_, z_, c_), "expert": e_}

    sibling = dev(xl, z, oc, e)
    ring = (dev(xl, mod(z + 1, NZ), c, e), dev(xl, mod(z - 1, NZ), c, e))
    me16 = e * 2 + c
    me32 = (xl * 2 + c) * NE + e

    def peer16(m):
        e_ = m // 2
        xl_ = jnp.where(e_ // (NE // 2) == e // (NE // 2), xl, oxl)
        return dev(xl_, z, lax.rem(m, 2), e_)

    def peer32(m):
        return dev(m // (2 * NE), z, lax.rem(m // NE, 2), lax.rem(m, NE))

    def remote(src, dst, send, recv, device):
        return pltpu.make_async_remote_copy(
            src_ref=src, dst_ref=dst, send_sem=send, recv_sem=recv,
            device_id=device, device_id_type=MESH,
        )

    barrier = pltpu.get_barrier_semaphore()
    for d in range(2):
        pl.semaphore_signal(barrier, inc=1, device_id=ring[d], device_id_type=MESH)

    @pl.loop(1, GROUP)
    def _(k):
        pl.semaphore_signal(
            barrier, inc=1, device_id=peer32(lax.rem(me32 + k, GROUP)), device_id_type=MESH
        )

    def up_rows(dp_, count):
        return pl.ds(pl.multiple_of(dp_ * UPR, 16), count)

    def down_rows(dp_, count):
        return pl.ds(pl.multiple_of(dp_ * DNR, 16), count)

    def tok_rows(block):
        return pl.ds(pl.multiple_of(block * TOK, TOK), TOK)

    def half_cols(order, q):
        return pl.ds(pl.multiple_of(order * HALF + q * QW, 128), QW)

    up_buf[up_rows(dp, UPR), :] = up_ref[c]
    down_buf[down_rows(dp, DNR), :] = down_ref[c]
    mine, theirs = z * 2 + c, z * 2 + oc
    mbuf[mine] = mmeta_ref[c]
    for q in range(Q):
        gbuf[q, tok_rows(mine), :] = grad_ref[:, half_cols(c, q)]

    ids = (emeta_ref[0:1, :], emeta_ref[1:2, :])
    gates = (emeta_ref[2:3, :], emeta_ref[3:4, :])
    numbers = lax.broadcasted_iota(jnp.int32, (EXPERTS, TOK), 0).astype(F32)
    zeros = jnp.zeros((EXPERTS, TOK), F32)
    hit0, hit1 = numbers == ids[0], numbers == ids[1]
    hits = jnp.where(hit0 | hit1, 1.0, 0.0)
    weight = jnp.where(hit0, gates[0], zeros) + jnp.where(hit1, gates[1], zeros)
    earlier = jnp.where(
        lax.broadcasted_iota(jnp.int32, (TOK, TOK), 0)
        < lax.broadcasted_iota(jnp.int32, (TOK, TOK), 1),
        1.0, 0.0,
    ).astype(BF16)
    rank = jnp.dot(hits.astype(BF16), earlier, preferred_element_type=F32)
    place = jnp.where(hits > 0.5, rank, -1.0)
    slots = lax.broadcasted_iota(jnp.int32, (CAP, TOK), 0).astype(F32)
    for x in range(EXPERTS):
        chosen = slots == place[x : x + 1, :]
        pick[x * CAP : (x + 1) * CAP, :] = jnp.where(chosen, 1.0, 0.0).astype(BF16)
        blend[x * CAP : (x + 1) * CAP, :] = jnp.where(chosen, weight[x : x + 1, :], 0.0)

    own = me16 // 4

    def dispatch(i):
        first = lax.rem(own + i, 4) * 4
        rows = pl.ds(pl.multiple_of(first * CAP, 128), 4 * CAP)
        onehot = pick[rows, :]

        @pl.loop(0, 5)
        def _(n):
            cols = pl.ds(pl.multiple_of(n * 512, 512), 512)
            send_x[rows, cols] = jnp.dot(
                onehot, input_ref[:, cols], preferred_element_type=F32
            ).astype(BF16)
            send_g[rows, cols] = jnp.dot(
                onehot, grad_ref[:, cols], preferred_element_type=F32
            ).astype(BF16)

    def slot_rows(m):
        return pl.ds(pl.multiple_of(m * CAP, CAP), CAP)

    def dispatch_sends(i):
        @pl.loop(0, 4)
        def _(k):
            m = lax.rem(own + i, 4) * 4 + lax.rem(me16 + k, 4)

            @pl.when(m != me16)
            def _():
                remote(
                    send_x.at[slot_rows(m)], got_x.at[slot_rows(me16)],
                    d_send.at[0], d_recv.at[0], peer16(m),
                ).start()
                remote(
                    send_g.at[slot_rows(m)], got_g.at[slot_rows(me16)],
                    d_send.at[1], d_recv.at[1], peer16(m),
                ).start()

    dispatch(1)
    pl.semaphore_wait(barrier, GROUP - 1 + 2)

    pre = [
        remote(up_ref.at[oc], up_buf.at[up_rows(dp, UPR)], pre_send.at[0], pre_recv.at[0], sibling),
        remote(
            down_ref.at[oc], down_buf.at[down_rows(dp, DNR)],
            pre_send.at[1], pre_recv.at[1], sibling,
        ),
        remote(mmeta_ref.at[oc], mbuf.at[mine], pre_send.at[2], pre_recv.at[2], sibling),
    ]
    for q in range(Q):
        pre.append(remote(
            grad_ref.at[:, half_cols(oc, q)], gbuf.at[q, tok_rows(mine)],
            pre_send.at[3 + q], pre_recv.at[3 + q], sibling,
        ))
    arrivals = [
        up_buf.at[up_rows(dp_of(xl, z, oc), UPR)],
        down_buf.at[down_rows(dp_of(xl, z, oc), DNR)],
        mbuf.at[theirs],
    ]
    for q in range(Q):
        arrivals.append(gbuf.at[q, tok_rows(theirs)])

    def pre_wait(at):
        remote(arrivals[at], arrivals[at], pre_send.at[at], pre_recv.at[at], sibling).wait_recv()

    def origin(d, s):
        return mod(z - s, NZ) if d == 0 else mod(z + s, NZ)

    def ring_block(kind, d, zs):
        if kind == "weights":
            if d == 0:
                return up_buf.at[up_rows(dp_of(xl, zs, 0), 2 * UPR)]
            return down_buf.at[down_rows(dp_of(xl, zs, 0), 2 * DNR)]
        block = zs * 2 + (c, oc)[d]
        if kind == "meta":
            return mbuf.at[block]
        return gbuf.at[kind, tok_rows(block)]

    def ring_sems(kind, d, s):
        if kind == "weights":
            return w_send.at[d], w_recv.at[d, s]
        if kind == "meta":
            return m_send, m_recv.at[d, s]
        return t_send.at[kind], t_recv.at[d, kind, s]

    def ring_send(kind, d, s):
        block = ring_block(kind, d, origin(d, s))
        send, recv = ring_sems(kind, d, s)
        remote(block, block, send, recv, ring[d]).start()

    def ring_wait(kind, d, s):
        block = ring_block(kind, d, origin(d, s + 1))
        send, recv = ring_sems(kind, d, s)
        remote(block, block, send, recv, ring[d]).wait_recv()

    across = dev(oxl, z, c, e)

    def cross(d, zs):
        block = ring_block("weights", d, zs)
        remote(block, block, x_send.at[d], x_recv.at[d], across).start()

    def ring_step(kinds, s):
        for kind in kinds:
            for d in range(2):
                ring_wait(kind, d, s - 1)
                if s < NZ - 1:
                    ring_send(kind, d, s)
                if kind == "weights":
                    cross(d, origin(d, s))

    remote(
        up_ref.at[c], up_buf.at[up_rows(dp, UPR)], w_send.at[0], w_recv.at[0, 0], ring[0]
    ).start()
    remote(
        down_ref.at[c], down_buf.at[down_rows(dp, DNR)], w_send.at[1], w_recv.at[1, 0], ring[1]
    ).start()
    for copy in pre[:5]:
        copy.start()
    ring_send(0, 0, 0)
    ring_send(1, 0, 0)
    dispatch_sends(1)
    dispatch(2)
    pre_wait(0)
    remote(
        arrivals[0], arrivals[0], w_send.at[0], w_recv.at[0, 0], ring[0]
    ).start()
    cross(0, z)
    pre_wait(1)
    remote(
        arrivals[1], arrivals[1], w_send.at[1], w_recv.at[1, 0], ring[1]
    ).start()
    cross(1, z)
    pre_wait(2)
    for d in range(2):
        ring_send("meta", d, 0)
    for q in range(2):
        pre_wait(3 + q)
        ring_send(q, 1, 0)
    dispatch_sends(2)
    for copy in pre[5:]:
        copy.start()
    for i in (3, 0):
        dispatch(i)
        dispatch_sends(i)
    got_x[slot_rows(me16), :] = send_x[slot_rows(me16), :]
    got_g[slot_rows(me16), :] = send_g[slot_rows(me16), :]

    for s in range(1, NZ):
        ring_step(("weights", 0, 1, "meta"), s)
    for q in range(2, Q):
        pre_wait(3 + q)
        for d in range(2):
            ring_send(q, d, 0)

    def all_bytes(ref, sem):
        pltpu.make_async_copy(ref, ref, sem).wait()

    some = pl.ds(0, (EXPERTS - 1) * CAP)

    def expert(i):
        rows = pl.ds(i * 256, 256)

        @pl.loop(0, 2)
        def _(n):
            cols = pl.ds(pl.multiple_of(n * 256, 256), 256)
            before = jnp.dot(got_x[rows, :], up_buf[:, cols], preferred_element_type=F32)
            back = nt_dot(got_g[rows, :], down_buf[cols, :])
            sig = 1.0 / (1.0 + jnp.exp(-before))
            slope_buf[:, cols] = (back * sig * (1.0 + before * (1.0 - sig))).astype(BF16)

        @pl.loop(0, D // 256)
        def _(n):
            cols = pl.ds(pl.multiple_of(n * 256, 256), 256)
            ret_send[rows, cols] = nt_dot(slope_buf[...], up_buf[cols, :]).astype(BF16)

        @pl.loop(0, 8)
        def _(k):
            m = i * 8 + lax.rem(me16 + k, 8)

            @pl.when(m != me16)
            def _():
                remote(
                    ret_send.at[slot_rows(m)], ret_got.at[slot_rows(me16)],
                    r_send, r_recv, peer16(m),
                ).start()

    targets = (lax.broadcasted_iota(jnp.int32, (TROWS, TOK), 0) + z * TROWS).astype(F32)

    def select(block):
        cols = pl.ds(pl.multiple_of(block * TOK, TOK), TOK)
        meta = mbuf[block]
        one = jnp.where(targets == meta[1:2, :], meta[3:4, :], 0.0)
        sel[:, cols] = jnp.where(targets == meta[0:1, :], meta[2:3, :], one).astype(BF16)

    def table_rows(m):
        return pl.ds(pl.multiple_of(m * 32, 32), 32)

    def table_part(q):
        @pl.loop(0, TROWS // 256)
        def _(i):
            rows = pl.ds(pl.multiple_of(i * 256, 256), 256)
            dense[q, rows, :] = jnp.dot(
                sel[rows, :], gbuf[q], preferred_element_type=F32
            ).astype(BF16)

        @pl.loop(1, GROUP)
        def _(k):
            m = lax.rem(me32 + k, GROUP)
            remote(
                dense.at[q, table_rows(m)], rs_got.at[q, (c * 2 + xl) * NE + e],
                rs_send.at[q], rs_recv.at[q], peer32(m),
            ).start()

        rs_got[q, (c * 2 + xl) * NE + e] = dense[q, table_rows(me32), :]

    def table_sum(q):
        all_bytes(rs_got.at[q, pl.ds(0, GROUP - 1)], rs_recv.at[q])
        for order in range(2):
            total = rs_got[q, order * 16].astype(F32)
            for k in range(1, 16):
                total += rs_got[q, order * 16 + k].astype(F32)
            table_ref[order * 2 : order * 2 + 2, :, q * QW : (q + 1) * QW] = total.reshape(
                2, 16, QW
            )

    last = tuple(range(2, Q))
    pl.loop(0, BLOCKS // 2)(select)
    ring_step(last, 1)
    pl.loop(BLOCKS // 2, BLOCKS)(select)
    ring_step(last, 2)
    table_part(0)
    table_part(1)
    ring_step(last, 3)
    all_bytes(up_buf.at[up_rows(dp_of(oxl, 0, 0), NZ * 2 * UPR)], x_recv.at[0])
    all_bytes(down_buf.at[down_rows(dp_of(oxl, 0, 0), NZ * 2 * DNR)], x_recv.at[1])
    all_bytes(got_x.at[some], d_recv.at[0])
    all_bytes(got_g.at[some], d_recv.at[1])
    expert(0)
    ring_step(last, 4)
    expert(1)
    ret_got[slot_rows(me16), :] = ret_send[slot_rows(me16), :]
    for s in range(5, NZ):
        ring_step(last, s)
    for q in last:
        table_part(q)

    all_bytes(ret_got.at[some], r_recv)
    mix = blend[...].T.astype(BF16)

    @pl.loop(0, D // 256)
    def _(n):
        cols = pl.ds(pl.multiple_of(n * 256, 256), 256)
        gi_ref[:, cols] = jnp.dot(mix, ret_got[:, cols], preferred_element_type=F32).astype(BF16)

    for q in range(Q):
        table_sum(q)

    for copy in pre:
        copy.wait_send()
    sends = 2 * (NZ - 1)
    all_bytes(up_buf.at[pl.ds(0, (NZ - 1) * 2 * UPR)], w_send.at[0])
    all_bytes(down_buf.at[pl.ds(0, (NZ - 1) * 2 * DNR)], w_send.at[1])
    all_bytes(up_buf.at[pl.ds(0, NZ * 2 * UPR)], x_send.at[0])
    all_bytes(down_buf.at[pl.ds(0, NZ * 2 * DNR)], x_send.at[1])
    all_bytes(mbuf.at[pl.ds(0, sends)], m_send)
    for q in range(Q):
        all_bytes(gbuf.at[q, pl.ds(0, sends * TOK)], t_send.at[q])
        all_bytes(dense.at[q, pl.ds(0, (GROUP - 1) * 32)], rs_send.at[q])
    all_bytes(send_x.at[some], d_send.at[0])
    all_bytes(send_g.at[some], d_send.at[1])
    all_bytes(ret_send.at[some], r_send)


def per_device(
    grad_out, saved_input, expert_ids, gate_weights, up_weight, down_weight,
    engram_gate, memory_owner, memory_slot,
):
    emeta = jnp.concatenate(
        [expert_ids.astype(F32).T, gate_weights.T, jnp.zeros((4, TOK), F32)], axis=0
    )
    head = jnp.arange(4, dtype=jnp.int32)[None, :] % 2
    core = memory_owner % 2
    zs = (memory_owner // 2) % NZ
    xs = memory_owner // (2 * NZ)
    row = (((zs * XL + xs) * 2 + core) * NE + memory_slot // 16) * 32
    row = row + head * 16 + memory_slot % 16
    rows_t = row.astype(F32).T.reshape(2, 2, TOK)
    gates_t = engram_gate.T.reshape(2, 2, TOK)
    mmeta = jnp.concatenate([rows_t, gates_t, jnp.zeros((2, 4, TOK), F32)], axis=1)

    vmem = pl.BlockSpec(memory_space=pltpu.VMEM)
    dma = pltpu.SemaphoreType.DMA
    return pl.pallas_call(
        kernel,
        out_shape=(
            jax.ShapeDtypeStruct((TOK, D), BF16),
            jax.ShapeDtypeStruct((4, 16, HALF), F32),
        ),
        in_specs=[vmem] * 6,
        out_specs=(vmem, vmem),
        scratch_shapes=[
            pltpu.VMEM((D, HID), BF16),
            pltpu.VMEM((HID, D), BF16),
            pltpu.VMEM((EXPERTS * CAP, TOK), BF16),
            pltpu.VMEM((EXPERTS * CAP, TOK), F32),
            pltpu.VMEM((EXPERTS * CAP, D), BF16),
            pltpu.VMEM((EXPERTS * CAP, D), BF16),
            pltpu.VMEM((EXPERTS * CAP, D), BF16),
            pltpu.VMEM((EXPERTS * CAP, D), BF16),
            pltpu.VMEM((256, HID), BF16),
            pltpu.VMEM((EXPERTS * CAP, D), BF16),
            pltpu.VMEM((EXPERTS * CAP, D), BF16),
            pltpu.VMEM((Q, BLOCKS * TOK, QW), BF16),
            pltpu.VMEM((BLOCKS, 8, TOK), F32),
            pltpu.VMEM((TROWS, BLOCKS * TOK), BF16),
            pltpu.VMEM((Q, TROWS, QW), BF16),
            pltpu.VMEM((Q, GROUP, 32, QW), BF16),
            dma((3 + Q,)),
            dma((3 + Q,)),
            dma((2, NZ - 1)),
            dma((2,)),
            dma((2,)),
            dma((2,)),
            dma((2, NZ - 1)),
            dma(()),
            dma((2, Q, NZ - 1)),
            dma((Q,)),
            dma((2,)),
            dma((2,)),
            dma(()),
            dma(()),
            dma((Q,)),
            dma((Q,)),
        ],
        compiler_params=pltpu.CompilerParams(
            collective_id=0, has_side_effects=True, vmem_limit_bytes=58 * 1024 * 1024
        ),
        cost_estimate=pl.CostEstimate(
            flops=10_000_000_000, bytes_accessed=4_000_000, transcendentals=262_144
        ),
    )(grad_out, saved_input, up_weight, down_weight, emeta, mmeta)


def solution(mesh):
    tokens = P(("dp", "expert"), None)
    return jax.shard_map(
        per_device,
        mesh=mesh,
        in_specs=(
            tokens, tokens, tokens, tokens,
            P("expert", "dp", None), P("expert", "dp", None),
            tokens, tokens, tokens,
        ),
        out_specs=(tokens, P(None, ("dp", "expert"), None)),
        check_vma=False,
    )
```

```python
import functools

import jax
import jax.numpy as jnp
from jax import lax
from jax.experimental import pallas as pl
from jax.experimental.pallas import tpu as pltpu
from jax.sharding import PartitionSpec as P

MESH = pl.DeviceIdType.MESH
F32 = jnp.float32
BF16 = jnp.bfloat16
NZ = 8
XL = 2
CORES = 2
XH = 2
NY = 4
NE = XH * NY
NX = XH * XL
PEERS = NY * CORES
EXPERTS = NE * CORES
TOK = 128
D = 2560
HID = 512
CAP = 32
HALF = D // 2
Q = 5
QW = HALF // Q
UPR = D // (XL * NZ * CORES)
DNR = HID // (XL * NZ * CORES)
BLOCKS = NZ * CORES
XROWS = PEERS * 2 * 16
TROWS = NX * XROWS
SET = PEERS * CAP


def mod(value, size):
    return lax.rem(value + size, size)


def nt_dot(a, b):
    return lax.dot_general(a, b, (((1,), (1,)), ((), ())), preferred_element_type=F32)


def kernel(
    grad_ref, input_ref, up_ref, down_ref, emeta_ref, mmeta_ref,
    gi_ref, table_ref,
    up_buf, down_buf, far_x, far_g, far_meta, pick, far_pick, blend,
    send_x, send_g, got_x, got_g, slope_buf, ret_send, ret_got,
    gbuf, mbuf, sel, dense, s1_got, s2_send, s2_got,
    pre_recv, pre_send, w_recv, w_send, x_recv, x_send, m_recv, m_send, t_recv, t_send,
    f_recv, f_send, d_recv, d_send, r_recv, r_send, s1_recv, s1_send, s2_recv, s2_send_sem,
):
    dp = lax.axis_index("dp")
    e = lax.axis_index("expert")
    c = lax.rem(dp, 2)
    z = lax.rem(dp // 2, NZ)
    xl = dp // (2 * NZ)
    xh, y = e // NY, lax.rem(e, NY)
    x = xh * 2 + xl
    oc, oxl = 1 - c, 1 - xl

    def dp_of(xl_, z_, c_):
        return (xl_ * NZ + z_) * 2 + c_

    def dev(x_, y_, z_, c_):
        return {"dp": dp_of(lax.rem(x_, 2), z_, c_), "expert": (x_ // 2) * NY + y_}

    sibling = dev(x, y, z, oc)
    ring = (dev(x, y, mod(z + 1, NZ), c), dev(x, y, mod(z - 1, NZ), c))
    across = dev(xh * 2 + 1 - xl, y, z, c)
    far_xpos = NX - 1 - x
    far = dev(far_xpos, y, z, c)
    me16 = e * 2 + c
    me8 = y * 2 + c
    near = [(1, 0), (3, 0), (2, 0), (1, 1), (3, 1), (2, 1), (0, 1)]

    def near_at(dy, dc):
        return lax.rem(y + dy, NY), (oc if dc else c)

    def remote(src, dst, send, recv, device):
        return pltpu.make_async_remote_copy(
            src_ref=src, dst_ref=dst, send_sem=send, recv_sem=recv,
            device_id=device, device_id_type=MESH,
        )

    barrier = pltpu.get_barrier_semaphore()
    friends = list(ring)
    for dx in range(1, NX):
        friends.append(dev(lax.rem(x + dx, NX), y, z, c))
    for dy, dc in near:
        y_, c_ = near_at(dy, dc)
        friends.append(dev(x, y_, z, c_))
        friends.append(dev(far_xpos, y_, z, c_))
    for friend in friends:
        pl.semaphore_signal(barrier, inc=1, device_id=friend, device_id_type=MESH)

    def up_rows(dp_, count):
        return pl.ds(pl.multiple_of(dp_ * UPR, 16), count)

    def down_rows(dp_, count):
        return pl.ds(pl.multiple_of(dp_ * DNR, 16), count)

    def tok_rows(block):
        return pl.ds(pl.multiple_of(block * TOK, TOK), TOK)

    def half_cols(order, q):
        return pl.ds(pl.multiple_of(order * HALF + q * QW, 128), QW)

    up_buf[up_rows(dp, UPR), :] = up_ref[c]
    down_buf[down_rows(dp, DNR), :] = down_ref[c]
    mine, theirs = z * 2 + c, z * 2 + oc
    mbuf[mine] = mmeta_ref[c]
    for q in range(Q):
        gbuf[q, tok_rows(mine), :] = grad_ref[:, half_cols(c, q)]

    numbers = lax.broadcasted_iota(jnp.int32, (EXPERTS, TOK), 0).astype(F32)
    zeros = jnp.zeros((EXPERTS, TOK), F32)
    earlier = jnp.where(
        lax.broadcasted_iota(jnp.int32, (TOK, TOK), 0)
        < lax.broadcasted_iota(jnp.int32, (TOK, TOK), 1),
        1.0, 0.0,
    ).astype(BF16)
    slots = lax.broadcasted_iota(jnp.int32, (CAP, TOK), 0).astype(F32)

    def choose(meta, pick_ref, blend_ref):
        hit0, hit1 = numbers == meta[0:1, :], numbers == meta[1:2, :]
        hits = jnp.where(hit0 | hit1, 1.0, 0.0)
        weight = jnp.where(hit0, meta[2:3, :], zeros) + jnp.where(hit1, meta[3:4, :], zeros)
        rank = jnp.dot(hits.astype(BF16), earlier, preferred_element_type=F32)
        place = jnp.where(hits > 0.5, rank, -1.0)
        for n in range(EXPERTS):
            chosen = slots == place[n : n + 1, :]
            rows = slice(n * CAP, (n + 1) * CAP)
            pick_ref[rows, :] = jnp.where(chosen, 1.0, 0.0).astype(BF16)
            if blend_ref is not None:
                blend_ref[rows, :] = jnp.where(chosen, weight[n : n + 1, :], 0.0)

    def dispatch(group, array):
        pick_ref = (pick, far_pick)[group]
        src = ((input_ref, grad_ref), (far_x, far_g))[group][array]
        out = (send_x, send_g)[array]
        onehot = pick_ref[pl.ds(pl.multiple_of(xh * SET, SET), SET), :]

        @pl.loop(0, 5)
        def _(n):
            cols = pl.ds(pl.multiple_of(n * 512, 512), 512)
            out[group * SET : (group + 1) * SET, cols] = jnp.dot(
                onehot, src[:, cols], preferred_element_type=F32
            ).astype(BF16)

    def slot_rows(group, m):
        return pl.ds(pl.multiple_of(group * SET + m * CAP, CAP), CAP)

    def dispatch_sends(group, array):
        out, got = ((send_x, got_x), (send_g, got_g))[array]
        for dy, dc in near:
            y_, c_ = near_at(dy, dc)
            remote(
                out.at[slot_rows(group, y_ * 2 + c_)], got.at[slot_rows(group, me8)],
                d_send.at[group, array], d_recv.at[group, array], dev(x, y_, z, c_),
            ).start()
        got[slot_rows(group, me8), :] = out[slot_rows(group, me8), :]

    choose(emeta_ref[...], pick, blend)
    dispatch(0, 0)
    pl.semaphore_wait(barrier, len(friends))

    pre = [
        remote(up_ref.at[oc], up_buf.at[up_rows(dp, UPR)], pre_send.at[0], pre_recv.at[0], sibling),
        remote(
            down_ref.at[oc], down_buf.at[down_rows(dp, DNR)],
            pre_send.at[1], pre_recv.at[1], sibling,
        ),
        remote(mmeta_ref.at[oc], mbuf.at[mine], pre_send.at[2], pre_recv.at[2], sibling),
    ]
    for q in range(Q):
        pre.append(remote(
            grad_ref.at[:, half_cols(oc, q)], gbuf.at[q, tok_rows(mine)],
            pre_send.at[3 + q], pre_recv.at[3 + q], sibling,
        ))
    arrivals = [
        up_buf.at[up_rows(dp_of(xl, z, oc), UPR)],
        down_buf.at[down_rows(dp_of(xl, z, oc), DNR)],
        mbuf.at[theirs],
    ]
    for q in range(Q):
        arrivals.append(gbuf.at[q, tok_rows(theirs)])

    def pre_wait(at):
        remote(arrivals[at], arrivals[at], pre_send.at[at], pre_recv.at[at], sibling).wait_recv()

    def origin(d, s):
        return mod(z - s, NZ) if d == 0 else mod(z + s, NZ)

    def ring_block(kind, d, zs):
        if kind == "weights":
            if d == 0:
                return up_buf.at[up_rows(dp_of(xl, zs, 0), 2 * UPR)]
            return down_buf.at[down_rows(dp_of(xl, zs, 0), 2 * DNR)]
        block = zs * 2 + (c, oc)[d]
        if kind == "meta":
            return mbuf.at[block]
        return gbuf.at[kind, tok_rows(block)]

    def ring_sems(kind, d, s):
        if kind == "weights":
            return w_send.at[d], w_recv.at[d, s]
        if kind == "meta":
            return m_send, m_recv.at[d, s]
        return t_send.at[kind], t_recv.at[d, kind, s]

    def ring_send(kind, d, s):
        block = ring_block(kind, d, origin(d, s))
        send, recv = ring_sems(kind, d, s)
        remote(block, block, send, recv, ring[d]).start()

    def ring_wait(kind, d, s):
        block = ring_block(kind, d, origin(d, s + 1))
        send, recv = ring_sems(kind, d, s)
        remote(block, block, send, recv, ring[d]).wait_recv()

    def cross(d, zs):
        block = ring_block("weights", d, zs)
        remote(block, block, x_send.at[d], x_recv.at[d], across).start()

    def ring_step(kinds, s):
        for kind in kinds:
            for d in range(2):
                ring_wait(kind, d, s - 1)
                if s < NZ - 1:
                    ring_send(kind, d, s)
                if kind == "weights":
                    cross(d, origin(d, s))

    def far_copy(at):
        src, dst = ((input_ref, far_x), (emeta_ref, far_meta), (grad_ref, far_g))[at]
        return remote(src, dst, f_send.at[at], f_recv.at[at], far)

    remote(
        up_ref.at[c], up_buf.at[up_rows(dp, UPR)], w_send.at[0], w_recv.at[0, 0], ring[0]
    ).start()
    remote(
        down_ref.at[c], down_buf.at[down_rows(dp, DNR)], w_send.at[1], w_recv.at[1, 0], ring[1]
    ).start()
    for copy in pre[:5]:
        copy.start()
    for at in range(3):
        far_copy(at).start()
    ring_send(0, 0, 0)
    ring_send(1, 0, 0)
    dispatch_sends(0, 0)
    dispatch(0, 1)
    dispatch_sends(0, 1)
    pre_wait(0)
    remote(
        arrivals[0], arrivals[0], w_send.at[0], w_recv.at[0, 0], ring[0]
    ).start()
    cross(0, z)
    pre_wait(1)
    remote(
        arrivals[1], arrivals[1], w_send.at[1], w_recv.at[1, 0], ring[1]
    ).start()
    cross(1, z)
    pre_wait(2)
    for d in range(2):
        ring_send("meta", d, 0)
    for q in range(2):
        pre_wait(3 + q)
        ring_send(q, 1, 0)
    for copy in pre[5:]:
        copy.start()

    first = ("weights", 0, 1, "meta")
    ring_step(first, 1)
    ring_step(first, 2)
    far_copy(0).wait_recv()
    far_copy(1).wait_recv()
    choose(far_meta[...], far_pick, None)
    dispatch(1, 0)
    dispatch_sends(1, 0)
    ring_step(first, 3)
    ring_step(first, 4)
    far_copy(2).wait_recv()
    dispatch(1, 1)
    dispatch_sends(1, 1)
    for s in range(5, NZ):
        ring_step(first, s)
    for q in range(2, Q):
        pre_wait(3 + q)
        for d in range(2):
            ring_send(q, d, 0)

    def all_bytes(ref, sem):
        pltpu.make_async_copy(ref, ref, sem).wait()

    def others(group):
        return pl.ds(group * SET, (PEERS - 1) * CAP)

    def expert(group):
        all_bytes(got_x.at[others(group)], d_recv.at[group, 0])
        all_bytes(got_g.at[others(group)], d_recv.at[group, 1])
        rows = pl.ds(group * SET, SET)

        @pl.loop(0, 2)
        def _(n):
            cols = pl.ds(pl.multiple_of(n * 256, 256), 256)
            before = jnp.dot(got_x[rows, :], up_buf[:, cols], preferred_element_type=F32)
            back = nt_dot(got_g[rows, :], down_buf[cols, :])
            sig = 1.0 / (1.0 + jnp.exp(-before))
            slope_buf[:, cols] = (back * sig * (1.0 + before * (1.0 - sig))).astype(BF16)

        @pl.loop(0, D // 256)
        def _(n):
            cols = pl.ds(pl.multiple_of(n * 256, 256), 256)
            ret_send[rows, cols] = nt_dot(slope_buf[...], up_buf[cols, :]).astype(BF16)

        back_to = pl.ds(pl.multiple_of(me16 * CAP, CAP), CAP)
        for dy, dc in near + ([(0, 0)] if group else []):
            y_, c_ = near_at(dy, dc)
            remote(
                ret_send.at[slot_rows(group, y_ * 2 + c_)], ret_got.at[back_to],
                r_send, r_recv, dev((x, far_xpos)[group], y_, z, c_),
            ).start()
        if group == 0:
            ret_got[back_to, :] = ret_send[slot_rows(group, me8), :]

    targets = (lax.broadcasted_iota(jnp.int32, (TROWS, TOK), 0) + z * TROWS).astype(F32)

    def select(block):
        cols = pl.ds(pl.multiple_of(block * TOK, TOK), TOK)
        meta = mbuf[block]
        one = jnp.where(targets == meta[1:2, :], meta[3:4, :], 0.0)
        sel[:, cols] = jnp.where(targets == meta[0:1, :], meta[2:3, :], one).astype(BF16)

    def x_rows(x_):
        return pl.ds(pl.multiple_of(x_ * XROWS, XROWS), XROWS)

    def m_rows(m):
        return pl.ds(pl.multiple_of(m * 32, 32), 32)

    def table_part(q):
        @pl.loop(0, TROWS // 256)
        def _(i):
            rows = pl.ds(pl.multiple_of(i * 256, 256), 256)
            dense[q, rows, :] = jnp.dot(
                sel[rows, :], gbuf[q], preferred_element_type=F32
            ).astype(BF16)

        for dx in (1, 3, 2):
            x_ = lax.rem(x + dx, NX)
            remote(
                dense.at[q, x_rows(x_)], s1_got.at[q, dx - 1],
                s1_send.at[q], s1_recv.at[q], dev(x_, y, z, c),
            ).start()

    def table_mid(q):
        all_bytes(s1_got.at[q], s1_recv.at[q])
        total = dense[q, x_rows(x), :].astype(F32)
        for k in range(NX - 1):
            total += s1_got[q, k].astype(F32)
        s2_send[q] = total.astype(BF16)
        for dy, dc in near:
            y_, c_ = near_at(dy, dc)
            remote(
                s2_send.at[q, m_rows(y_ * 2 + c_)], s2_got.at[q, c * NY + y],
                s2_send_sem.at[q], s2_recv.at[q], dev(x, y_, z, c_),
            ).start()
        s2_got[q, c * NY + y] = s2_send[q, m_rows(me8), :]

    def table_sum(q):
        all_bytes(s2_got.at[q, pl.ds(0, PEERS - 1)], s2_recv.at[q])
        for order in range(2):
            total = s2_got[q, order * NY].astype(F32)
            for k in range(1, NY):
                total += s2_got[q, order * NY + k].astype(F32)
            table_ref[order * 2 : order * 2 + 2, :, q * QW : (q + 1) * QW] = total.reshape(
                2, 16, QW
            )

    last = tuple(range(2, Q))
    pl.loop(0, BLOCKS // 2)(select)
    ring_step(last, 1)
    pl.loop(BLOCKS // 2, BLOCKS)(select)
    ring_step(last, 2)
    table_part(0)
    table_part(1)
    ring_step(last, 3)
    all_bytes(up_buf.at[up_rows(dp_of(oxl, 0, 0), NZ * 2 * UPR)], x_recv.at[0])
    all_bytes(down_buf.at[down_rows(dp_of(oxl, 0, 0), NZ * 2 * DNR)], x_recv.at[1])
    expert(0)
    ring_step(last, 4)
    expert(1)
    for s in range(5, NZ):
        ring_step(last, s)
    for q in last:
        table_part(q)
    for q in range(Q):
        table_mid(q)

    all_bytes(ret_got.at[pl.ds(0, (EXPERTS - 1) * CAP)], r_recv)
    mix = blend[...].T.astype(BF16)

    @pl.loop(0, D // 256)
    def _(n):
        cols = pl.ds(pl.multiple_of(n * 256, 256), 256)
        gi_ref[:, cols] = jnp.dot(mix, ret_got[:, cols], preferred_element_type=F32).astype(BF16)

    for q in range(Q):
        table_sum(q)

    for copy in pre:
        copy.wait_send()
    sends = 2 * (NZ - 1)
    all_bytes(up_buf.at[pl.ds(0, (NZ - 1) * 2 * UPR)], w_send.at[0])
    all_bytes(down_buf.at[pl.ds(0, (NZ - 1) * 2 * DNR)], w_send.at[1])
    all_bytes(up_buf.at[pl.ds(0, NZ * 2 * UPR)], x_send.at[0])
    all_bytes(down_buf.at[pl.ds(0, NZ * 2 * DNR)], x_send.at[1])
    all_bytes(mbuf.at[pl.ds(0, sends)], m_send)
    for q in range(Q):
        all_bytes(gbuf.at[q, pl.ds(0, sends * TOK)], t_send.at[q])
        all_bytes(s1_got.at[q], s1_send.at[q])
        all_bytes(s2_got.at[q, pl.ds(0, PEERS - 1)], s2_send_sem.at[q])
    for at in range(3):
        far_copy(at).wait_send()
    for group in range(2):
        all_bytes(send_x.at[others(group)], d_send.at[group, 0])
        all_bytes(send_g.at[others(group)], d_send.at[group, 1])
    all_bytes(ret_send.at[pl.ds(0, (EXPERTS - 1) * CAP)], r_send)


def per_device(
    grad_out, saved_input, expert_ids, gate_weights, up_weight, down_weight,
    engram_gate, memory_owner, memory_slot,
):
    emeta = jnp.concatenate(
        [expert_ids.astype(F32).T, gate_weights.T, jnp.zeros((4, TOK), F32)], axis=0
    )
    head = jnp.arange(4, dtype=jnp.int32)[None, :] % 2
    core = memory_owner % 2
    zs = (memory_owner // 2) % NZ
    xs = memory_owner // (2 * NZ)
    to = memory_slot // 16
    xs = (to // NY) * 2 + xs
    row = (((zs * NX + xs) * NY + to % NY) * 2 + core) * 32
    row = row + head * 16 + memory_slot % 16
    rows_t = row.astype(F32).T.reshape(2, 2, TOK)
    gates_t = engram_gate.T.reshape(2, 2, TOK)
    mmeta = jnp.concatenate([rows_t, gates_t, jnp.zeros((2, 4, TOK), F32)], axis=1)

    vmem = pl.BlockSpec(memory_space=pltpu.VMEM)
    dma = pltpu.SemaphoreType.DMA
    return pl.pallas_call(
        kernel,
        out_shape=(
            jax.ShapeDtypeStruct((TOK, D), BF16),
            jax.ShapeDtypeStruct((4, 16, HALF), F32),
        ),
        in_specs=[vmem] * 6,
        out_specs=(vmem, vmem),
        scratch_shapes=[
            pltpu.VMEM((D, HID), BF16),
            pltpu.VMEM((HID, D), BF16),
            pltpu.VMEM((TOK, D), BF16),
            pltpu.VMEM((TOK, D), BF16),
            pltpu.VMEM((8, TOK), F32),
            pltpu.VMEM((EXPERTS * CAP, TOK), BF16),
            pltpu.VMEM((EXPERTS * CAP, TOK), BF16),
            pltpu.VMEM((EXPERTS * CAP, TOK), F32),
            pltpu.VMEM((EXPERTS * CAP, D), BF16),
            pltpu.VMEM((EXPERTS * CAP, D), BF16),
            pltpu.VMEM((EXPERTS * CAP, D), BF16),
            pltpu.VMEM((EXPERTS * CAP, D), BF16),
            pltpu.VMEM((256, HID), BF16),
            pltpu.VMEM((EXPERTS * CAP, D), BF16),
            pltpu.VMEM((EXPERTS * CAP, D), BF16),
            pltpu.VMEM((Q, BLOCKS * TOK, QW), BF16),
            pltpu.VMEM((BLOCKS, 8, TOK), F32),
            pltpu.VMEM((TROWS, BLOCKS * TOK), BF16),
            pltpu.VMEM((Q, TROWS, QW), BF16),
            pltpu.VMEM((Q, NX - 1, XROWS, QW), BF16),
            pltpu.VMEM((Q, XROWS, QW), BF16),
            pltpu.VMEM((Q, PEERS, 32, QW), BF16),
            dma((3 + Q,)),
            dma((3 + Q,)),
            dma((2, NZ - 1)),
            dma((2,)),
            dma((2,)),
            dma((2,)),
            dma((2, NZ - 1)),
            dma(()),
            dma((2, Q, NZ - 1)),
            dma((Q,)),
            dma((3,)),
            dma((3,)),
            dma((2, 2)),
            dma((2, 2)),
            dma(()),
            dma(()),
            dma((Q,)),
            dma((Q,)),
            dma((Q,)),
            dma((Q,)),
        ],
        compiler_params=pltpu.CompilerParams(
            collective_id=0, has_side_effects=True, vmem_limit_bytes=58 * 1024 * 1024
        ),
        cost_estimate=pl.CostEstimate(
            flops=10_000_000_000, bytes_accessed=4_000_000, transcendentals=262_144
        ),
    )(grad_out, saved_input, up_weight, down_weight, emeta, mmeta)


def solution(mesh):
    tokens = P(("dp", "expert"), None)
    return jax.shard_map(
        per_device,
        mesh=mesh,
        in_specs=(
            tokens, tokens, tokens, tokens,
            P("expert", "dp", None), P("expert", "dp", None),
            tokens, tokens, tokens,
        ),
        out_specs=(tokens, P(None, ("dp", "expert"), None)),
        check_vma=False,
    )
```

```python
import functools

import jax
import jax.numpy as jnp
from jax import lax
from jax.experimental import pallas as pl
from jax.experimental.pallas import tpu as pltpu
from jax.sharding import PartitionSpec as P

MESH = pl.DeviceIdType.MESH
F32 = jnp.float32
BF16 = jnp.bfloat16
NZ = 8
XL = 2
CORES = 2
FAR_Z = NZ // 2
XH = 2
NY = 4
NE = XH * NY
NX = XH * XL
PEERS = NY * CORES
EXPERTS = NE * CORES
TOK = 128
D = 2560
HID = 512
CAP = 32
HALF = D // 2
Q = 5
QW = HALF // Q
UPR = D // (XL * NZ * CORES)
DNR = HID // (XL * NZ * CORES)
BLOCKS = NZ * CORES
XROWS = PEERS * 2 * 16
TROWS = NX * XROWS
SET = PEERS * CAP


def mod(value, size):
    return lax.rem(value + size, size)


def nt_dot(a, b):
    return lax.dot_general(a, b, (((1,), (1,)), ((), ())), preferred_element_type=F32)


def kernel(
    grad_ref, input_ref, up_ref, down_ref, meta_ref,
    gi_ref, table_ref,
    up_buf, down_buf, far_x, far_g, far_meta, pick, far_pick, blend, far_blend,
    send_x, send_g, got_x, got_g, slope_buf, ret_send, ret_got, far_out, far_back,
    gbuf, mbuf, sel, dense, s1_got, s2_send, s2_got,
    pre_recv, pre_send, w_recv, w_send, x_recv, x2_recv, x_send, e_recv, e_send, m_recv, m_send, t_recv, t_send,
    f_recv, f_send, d_recv, d_send, r_recv, r_send, b_recv, b_send, s1_recv, s1_send, s2_recv, s2_send_sem,
):
    dp = lax.axis_index("dp")
    e = lax.axis_index("expert")
    c = lax.rem(dp, 2)
    z = lax.rem(dp // 2, NZ)
    xl = dp // (2 * NZ)
    xh, y = e // NY, lax.rem(e, NY)
    x = xh * 2 + xl
    oc, oxl = 1 - c, 1 - xl

    def dp_of(xl_, z_, c_):
        return (xl_ * NZ + z_) * 2 + c_

    def dev(x_, y_, z_, c_):
        return {"dp": dp_of(lax.rem(x_, 2), z_, c_), "expert": (x_ // 2) * NY + y_}

    sibling = dev(x, y, z, oc)
    ring = (dev(x, y, mod(z + 1, NZ), c), dev(x, y, mod(z - 1, NZ), c))
    across = dev(xh * 2 + 1 - xl, y, z, c)
    far = dev(NX - 1 - x, y, z, c)
    me8 = y * 2 + c
    near = [(1, 0), (3, 0), (2, 0), (1, 1), (3, 1), (2, 1), (0, 1)]

    def near_at(dy, dc):
        return lax.rem(y + dy, NY), (oc if dc else c)

    def remote(src, dst, send, recv, device):
        return pltpu.make_async_remote_copy(
            src_ref=src, dst_ref=dst, send_sem=send, recv_sem=recv,
            device_id=device, device_id_type=MESH,
        )

    barrier = pltpu.get_barrier_semaphore()
    friends = list(ring)
    for dx in range(1, NX):
        friends.append(dev(lax.rem(x + dx, NX), y, z, c))
    for dy, dc in near:
        y_, c_ = near_at(dy, dc)
        friends.append(dev(x, y_, z, c_))
    for friend in friends:
        pl.semaphore_signal(barrier, inc=1, device_id=friend, device_id_type=MESH)

    def up_rows(dp_, count):
        return pl.ds(pl.multiple_of(dp_ * UPR, 16), count)

    def down_rows(dp_, count):
        return pl.ds(pl.multiple_of(dp_ * DNR, 16), count)

    def tok_rows(block):
        return pl.ds(pl.multiple_of(block * TOK, TOK), TOK)

    def half_cols(order, q):
        return pl.ds(pl.multiple_of(order * HALF + q * QW, 128), QW)

    up_buf[up_rows(dp, UPR), :] = up_ref[c]
    down_buf[down_rows(dp, DNR), :] = down_ref[c]
    mine, theirs = z * 2 + c, z * 2 + oc
    mbuf[mine] = meta_ref[c]
    for q in range(Q):
        gbuf[q, tok_rows(mine), :] = grad_ref[:, half_cols(c, q)]

    numbers = lax.broadcasted_iota(jnp.int32, (EXPERTS, TOK), 0).astype(F32)
    zeros = jnp.zeros((EXPERTS, TOK), F32)
    earlier = jnp.where(
        lax.broadcasted_iota(jnp.int32, (TOK, TOK), 0)
        < lax.broadcasted_iota(jnp.int32, (TOK, TOK), 1),
        1.0, 0.0,
    ).astype(BF16)
    slots = lax.broadcasted_iota(jnp.int32, (CAP, TOK), 0).astype(F32)

    def choose(meta, pick_ref, blend_ref):
        hit0, hit1 = numbers == meta[0:1, :], numbers == meta[1:2, :]
        hits = jnp.where(hit0 | hit1, 1.0, 0.0)
        weight = jnp.where(hit0, meta[2:3, :], zeros) + jnp.where(hit1, meta[3:4, :], zeros)
        rank = jnp.dot(hits.astype(BF16), earlier, preferred_element_type=F32)
        place = jnp.where(hits > 0.5, rank, -1.0)
        for n in range(EXPERTS):
            chosen = slots == place[n : n + 1, :]
            rows = slice(n * CAP, (n + 1) * CAP)
            pick_ref[rows, :] = jnp.where(chosen, 1.0, 0.0).astype(BF16)
            blend_ref[rows, :] = jnp.where(chosen, weight[n : n + 1, :], 0.0)

    def dispatch(group, array):
        pick_ref = (pick, far_pick)[group]
        src = ((input_ref, grad_ref), (far_x, far_g))[group][array]
        out = (send_x, send_g)[array]
        onehot = pick_ref[pl.ds(pl.multiple_of(xh * SET, SET), SET), :]

        @pl.loop(0, 5)
        def _(n):
            cols = pl.ds(pl.multiple_of(n * 512, 512), 512)
            out[group * SET : (group + 1) * SET, cols] = jnp.dot(
                onehot, src[:, cols], preferred_element_type=F32
            ).astype(BF16)

    def slot_rows(group, m):
        return pl.ds(pl.multiple_of(group * SET + m * CAP, CAP), CAP)

    def dispatch_sends(group, array):
        out, got = ((send_x, got_x), (send_g, got_g))[array]
        for dy, dc in near:
            y_, c_ = near_at(dy, dc)
            remote(
                out.at[slot_rows(group, y_ * 2 + c_)], got.at[slot_rows(group, me8)],
                d_send.at[group, array], d_recv.at[group, array], dev(x, y_, z, c_),
            ).start()
        got[slot_rows(group, me8), :] = out[slot_rows(group, me8), :]

    choose(meta_ref[2], pick, blend)
    dispatch(0, 0)
    pl.semaphore_wait(barrier, len(friends))

    pre = [
        remote(up_ref.at[oc], up_buf.at[up_rows(dp, UPR)], pre_send.at[0], pre_recv.at[0], sibling),
        remote(
            down_ref.at[oc], down_buf.at[down_rows(dp, DNR)],
            pre_send.at[1], pre_recv.at[1], sibling,
        ),
        remote(meta_ref.at[oc], mbuf.at[mine], pre_send.at[2], pre_recv.at[2], sibling),
    ]
    for q in range(Q):
        pre.append(remote(
            grad_ref.at[:, half_cols(oc, q)], gbuf.at[q, tok_rows(mine)],
            pre_send.at[3 + q], pre_recv.at[3 + q], sibling,
        ))
    arrivals = [
        up_buf.at[up_rows(dp_of(xl, z, oc), UPR)],
        down_buf.at[down_rows(dp_of(xl, z, oc), DNR)],
        mbuf.at[theirs],
    ]
    for q in range(Q):
        arrivals.append(gbuf.at[q, tok_rows(theirs)])

    def pre_wait(at):
        remote(arrivals[at], arrivals[at], pre_send.at[at], pre_recv.at[at], sibling).wait_recv()

    def origin(d, s):
        return mod(z - s, NZ) if d == 0 else mod(z + s, NZ)

    def weight_rows(at, xl_, zs):
        dp_ = dp_of(xl_, zs, 0)
        if at == 0:
            return up_buf.at[up_rows(dp_, 2 * UPR)]
        return down_buf.at[down_rows(dp_, 2 * DNR)]

    def ring_parts(kind, d, s, half):
        zs = origin(d, s)
        if kind == "weights":
            return [
                (weight_rows(at, xl, zs), w_send.at[at], w_recv.at[d, at])
                for at in ((d,) if half else (0, 1))
            ]
        block, count = (zs * 2 + d, 1) if half else (zs * 2, 2)
        if kind == "meta":
            return [(mbuf.at[pl.ds(block, count)], m_send, m_recv.at[d])]
        rows = pl.ds(pl.multiple_of(block * TOK, TOK), count * TOK)
        return [(gbuf.at[kind, rows], t_send.at[kind], t_recv.at[d, kind])]

    def ring_send(kind, d, s):
        for block, send, recv in ring_parts(kind, d, s, s == FAR_Z - 1):
            remote(block, block, send, recv.at[s], ring[d]).start()

    def cross(block, at, recv):
        remote(block, block, x_send.at[at], recv, across).start()

    def ring_step(kind, s):
        for d in range(2):
            for block, send, recv in ring_parts(kind, d, s, s == FAR_Z):
                remote(block, block, send, recv.at[s - 1], ring[d]).wait_recv()
            if s < FAR_Z:
                ring_send(kind, d, s)
            if kind == "weights" and s != FAR_Z - 1:
                for at in (d,) if s == FAR_Z else (0, 1):
                    recv = x2_recv.at[at, d] if s == FAR_Z - 2 else x_recv.at[at]
                    cross(weight_rows(at, xl, origin(d, s)), at, recv)

    def wide_copy(d, at, s):
        block = weight_rows(at, oxl, origin(d, s))
        return remote(block, block, e_send.at[d, at], e_recv.at[d, at], ring[d])

    def wide_send(d):
        for at in range(2):
            block = weight_rows(at, oxl, origin(d, FAR_Z - 2))
            remote(block, block, x_send.at[at], x2_recv.at[at, d], across).wait_recv()
            wide_copy(d, at, FAR_Z - 2).start()

    def piece(q):
        pre_wait(3 + q)
        for d in range(2):
            ring_send(q, d, 0)

    def steps(*pairs):
        for kind, at in pairs:
            ring_step(kind, at)

    def far_copy(at):
        src, dst = ((input_ref, far_x), (meta_ref.at[2], far_meta), (grad_ref, far_g))[at]
        return remote(src, dst, f_send.at[at], f_recv.at[at], far)

    def set_out(at, block):
        for d in range(2):
            remote(block, block, w_send.at[at], w_recv.at[d, at, 0], ring[d]).start()
        cross(block, at, x_recv.at[at])

    for copy in pre[:3]:
        copy.start()
    set_out(0, up_buf.at[up_rows(dp, UPR)])
    set_out(1, down_buf.at[down_rows(dp, DNR)])
    for at in range(3):
        far_copy(at).start()
    pre_wait(0)
    set_out(0, arrivals[0])
    pre_wait(1)
    set_out(1, arrivals[1])
    dispatch_sends(0, 0)
    pre_wait(2)
    for d in range(2):
        ring_send("meta", d, 0)
    dispatch(0, 1)
    dispatch_sends(0, 1)
    for copy in pre[3:]:
        copy.start()

    targets = (lax.broadcasted_iota(jnp.int32, (TROWS, TOK), 0) + z * TROWS).astype(F32)

    def select(block):
        cols = pl.ds(pl.multiple_of(block * TOK, TOK), TOK)
        meta = mbuf[block]
        one = jnp.where(targets == meta[1:2, :], meta[3:4, :], 0.0)
        sel[:, cols] = jnp.where(targets == meta[0:1, :], meta[2:3, :], one).astype(BF16)

    def all_bytes(ref, sem):
        pltpu.make_async_copy(ref, ref, sem).wait()

    def others(group):
        return pl.ds(group * SET, (PEERS - 1) * CAP)

    def expert_in(group):
        all_bytes(got_x.at[others(group)], d_recv.at[group, 0])
        all_bytes(got_g.at[others(group)], d_recv.at[group, 1])
        rows = pl.ds(group * SET, SET)

        @pl.loop(0, 2)
        def _(n):
            cols = pl.ds(pl.multiple_of(n * 256, 256), 256)
            before = jnp.dot(got_x[rows, :], up_buf[:, cols], preferred_element_type=F32)
            back = nt_dot(got_g[rows, :], down_buf[cols, :])
            sig = 1.0 / (1.0 + jnp.exp(-before))
            slope_buf[:, cols] = (back * sig * (1.0 + before * (1.0 - sig))).astype(BF16)

    def expert_out(group, part):
        rows = pl.ds(group * SET, SET)

        @pl.loop(part * 5, part * 5 + 5)
        def _(n):
            cols = pl.ds(pl.multiple_of(n * 256, 256), 256)
            ret_send[rows, cols] = nt_dot(slope_buf[...], up_buf[cols, :]).astype(BF16)

        cols = slice(part * HALF, (part + 1) * HALF)
        for dy, dc in near:
            y_, c_ = near_at(dy, dc)
            remote(
                ret_send.at[slot_rows(group, y_ * 2 + c_), cols],
                ret_got.at[slot_rows(group, me8), cols],
                r_send.at[group, part], r_recv.at[group, part], dev(x, y_, z, c_),
            ).start()
        ret_got[slot_rows(group, me8), cols] = ret_send[slot_rows(group, me8), cols]

    def returned(group, part):
        cols = pl.ds(part * HALF, HALF)
        all_bytes(ret_got.at[others(group), cols], r_recv.at[group, part])

    def mix_of(blend_ref):
        return blend_ref[pl.ds(pl.multiple_of(xh * SET, SET), SET), :].T.astype(BF16)

    def back_copy(part):
        cols = pl.ds(part * HALF, HALF)
        return remote(
            far_out.at[:, cols], far_back.at[:, cols], b_send.at[part], b_recv.at[part], far
        )

    def far_combine(part):
        returned(1, part)
        mix = mix_of(far_blend)

        @pl.loop(part * 5, part * 5 + 5)
        def _(n):
            cols = pl.ds(pl.multiple_of(n * 256, 256), 256)
            far_out[:, cols] = jnp.dot(
                mix, ret_got[SET : 2 * SET, cols], preferred_element_type=F32
            ).astype(BF16)

        back_copy(part).start()

    def x_rows(x_):
        return pl.ds(pl.multiple_of(x_ * XROWS, XROWS), XROWS)

    def m_rows(m):
        return pl.ds(pl.multiple_of(m * 32, 32), 32)

    def table_part(q):
        @pl.loop(0, TROWS // 256)
        def _(i):
            rows = pl.ds(pl.multiple_of(i * 256, 256), 256)
            dense[q, rows, :] = jnp.dot(
                sel[rows, :], gbuf[q], preferred_element_type=F32
            ).astype(BF16)

        for dx in (1, 3, 2):
            x_ = lax.rem(x + dx, NX)
            remote(
                dense.at[q, x_rows(x_)], s1_got.at[q, dx - 1],
                s1_send.at[q], s1_recv.at[q], dev(x_, y, z, c),
            ).start()

    def table_mid(q):
        all_bytes(s1_got.at[q], s1_recv.at[q])
        total = dense[q, x_rows(x), :].astype(F32)
        for k in range(NX - 1):
            total += s1_got[q, k].astype(F32)
        s2_send[q] = total.astype(BF16)
        for dy, dc in near:
            y_, c_ = near_at(dy, dc)
            remote(
                s2_send.at[q, m_rows(y_ * 2 + c_)], s2_got.at[q, c * NY + y],
                s2_send_sem.at[q], s2_recv.at[q], dev(x, y_, z, c_),
            ).start()
        s2_got[q, c * NY + y] = s2_send[q, m_rows(me8), :]

    def table_sum(q):
        all_bytes(s2_got.at[q, pl.ds(0, PEERS - 1)], s2_recv.at[q])
        for order in range(2):
            total = s2_got[q, order * NY].astype(F32)
            for k in range(1, NY):
                total += s2_got[q, order * NY + k].astype(F32)
            table_ref[order * 2 : order * 2 + 2, :, q * QW : (q + 1) * QW] = total.reshape(
                2, 16, QW
            )

    def sources(s):
        for d in range(2):
            for core in range(2) if s < FAR_Z else (d,):
                select(origin(d, s) * 2 + core)

    steps(("weights", 1), ("meta", 1))
    select(mine)
    select(theirs)
    sources(1)
    steps(("weights", 2), ("meta", 2))
    far_copy(0).wait_recv()
    far_copy(1).wait_recv()
    choose(far_meta[...], far_pick, far_blend)
    dispatch(1, 0)
    dispatch_sends(1, 0)
    steps(("weights", 3), ("meta", 3))
    for q in range(3):
        piece(q)
    sources(2)
    far_copy(2).wait_recv()
    dispatch(1, 1)
    dispatch_sends(1, 1)
    steps(("weights", 4), ("meta", 4))
    wide_send(0)
    wide_send(1)
    steps((0, 1), (1, 1), (2, 1))
    sources(3)
    sources(4)
    all_bytes(up_buf.at[pl.ds(0, 4 * 2 * UPR)], x_recv.at[0])
    all_bytes(down_buf.at[pl.ds(0, 4 * 2 * DNR)], x_recv.at[1])
    for d in range(2):
        for at in range(2):
            wide_copy(d, at, FAR_Z - 1).wait_recv()
    expert_in(0)
    steps((0, 2), (1, 2), (2, 2))
    expert_out(0, 0)
    expert_out(0, 1)
    steps((0, 3), (1, 3), (2, 3))
    piece(3)
    piece(4)
    expert_in(1)
    expert_out(1, 0)
    expert_out(1, 1)
    for q in range(3):
        ring_step(q, 4)
        table_part(q)
    steps((3, 1), (4, 1))
    far_combine(0)
    steps((3, 2), (4, 2))
    table_mid(0)
    far_combine(1)
    steps((3, 3), (4, 3))
    table_mid(1)
    table_mid(2)
    for q in (3, 4):
        ring_step(q, 4)
        table_part(q)

    mix = mix_of(blend)
    for part in range(2):
        returned(0, part)
        back_copy(part).wait_recv()

        @pl.loop(part * 5, part * 5 + 5)
        def _(n):
            cols = pl.ds(pl.multiple_of(n * 256, 256), 256)
            total = jnp.dot(mix, ret_got[0:SET, cols], preferred_element_type=F32)
            gi_ref[:, cols] = (total + far_back[:, cols].astype(F32)).astype(BF16)

    for q in range(3):
        table_sum(q)
    table_mid(3)
    table_mid(4)
    table_sum(3)
    table_sum(4)

    for copy in pre:
        copy.wait_send()
    sends = 2 * (NZ - 1)
    all_bytes(up_buf.at[pl.ds(0, (NZ - 1) * 2 * UPR)], w_send.at[0])
    all_bytes(down_buf.at[pl.ds(0, (NZ - 1) * 2 * DNR)], w_send.at[1])
    all_bytes(up_buf.at[pl.ds(0, 6 * 2 * UPR)], x_send.at[0])
    all_bytes(down_buf.at[pl.ds(0, 6 * 2 * DNR)], x_send.at[1])
    for d in range(2):
        for at in range(2):
            wide_copy(d, at, FAR_Z - 2).wait_send()
    all_bytes(mbuf.at[pl.ds(0, sends)], m_send)
    for q in range(Q):
        all_bytes(gbuf.at[q, pl.ds(0, sends * TOK)], t_send.at[q])
        all_bytes(s1_got.at[q], s1_send.at[q])
        all_bytes(s2_got.at[q, pl.ds(0, PEERS - 1)], s2_send_sem.at[q])
    for at in range(3):
        far_copy(at).wait_send()
    for group in range(2):
        all_bytes(send_x.at[others(group)], d_send.at[group, 0])
        all_bytes(send_g.at[others(group)], d_send.at[group, 1])
        for part in range(2):
            all_bytes(ret_send.at[others(group), pl.ds(part * HALF, HALF)], r_send.at[group, part])
    for part in range(2):
        back_copy(part).wait_send()


def per_device(
    grad_out, saved_input, expert_ids, gate_weights, up_weight, down_weight,
    engram_gate, memory_owner, memory_slot,
):
    head = jnp.arange(4, dtype=jnp.int32)[None, :] % 2
    core = memory_owner % 2
    zs = (memory_owner // 2) % NZ
    xs = memory_owner // (2 * NZ)
    to = memory_slot // 16
    xs = (to // NY) * 2 + xs
    row = (((zs * NX + xs) * NY + to % NY) * 2 + core) * 32
    row = row + head * 16 + memory_slot % 16
    rows = jnp.concatenate([row, expert_ids], axis=1).astype(F32)
    gates = jnp.concatenate([engram_gate, gate_weights], axis=1)
    meta = jnp.concatenate(
        [
            rows.T.reshape(3, 2, TOK),
            gates.T.reshape(3, 2, TOK),
            jnp.zeros((3, 4, TOK), F32),
        ],
        axis=1,
    )

    vmem = pl.BlockSpec(memory_space=pltpu.VMEM)
    dma = pltpu.SemaphoreType.DMA
    return pl.pallas_call(
        kernel,
        out_shape=(
            jax.ShapeDtypeStruct((TOK, D), BF16),
            jax.ShapeDtypeStruct((4, 16, HALF), F32),
        ),
        in_specs=[vmem] * 5,
        out_specs=(vmem, vmem),
        scratch_shapes=[
            pltpu.VMEM((D, HID), BF16),
            pltpu.VMEM((HID, D), BF16),
            pltpu.VMEM((TOK, D), BF16),
            pltpu.VMEM((TOK, D), BF16),
            pltpu.VMEM((8, TOK), F32),
            pltpu.VMEM((EXPERTS * CAP, TOK), BF16),
            pltpu.VMEM((EXPERTS * CAP, TOK), BF16),
            pltpu.VMEM((EXPERTS * CAP, TOK), F32),
            pltpu.VMEM((EXPERTS * CAP, TOK), F32),
            pltpu.VMEM((EXPERTS * CAP, D), BF16),
            pltpu.VMEM((EXPERTS * CAP, D), BF16),
            pltpu.VMEM((EXPERTS * CAP, D), BF16),
            pltpu.VMEM((EXPERTS * CAP, D), BF16),
            pltpu.VMEM((256, HID), BF16),
            pltpu.VMEM((EXPERTS * CAP, D), BF16),
            pltpu.VMEM((EXPERTS * CAP, D), BF16),
            pltpu.VMEM((TOK, D), BF16),
            pltpu.VMEM((TOK, D), BF16),
            pltpu.VMEM((Q, BLOCKS * TOK, QW), BF16),
            pltpu.VMEM((BLOCKS, 8, TOK), F32),
            pltpu.VMEM((TROWS, BLOCKS * TOK), BF16),
            pltpu.VMEM((Q, TROWS, QW), BF16),
            pltpu.VMEM((Q, NX - 1, XROWS, QW), BF16),
            pltpu.VMEM((Q, XROWS, QW), BF16),
            pltpu.VMEM((Q, PEERS, 32, QW), BF16),
            dma((3 + Q,)),
            dma((3 + Q,)),
            dma((2, 2, FAR_Z)),
            dma((2,)),
            dma((2,)),
            dma((2, 2)),
            dma((2,)),
            dma((2, 2)),
            dma((2, 2)),
            dma((2, FAR_Z)),
            dma(()),
            dma((2, Q, FAR_Z)),
            dma((Q,)),
            dma((3,)),
            dma((3,)),
            dma((2, 2)),
            dma((2, 2)),
            dma((2, 2)),
            dma((2, 2)),
            dma((2,)),
            dma((2,)),
            dma((Q,)),
            dma((Q,)),
            dma((Q,)),
            dma((Q,)),
        ],
        compiler_params=pltpu.CompilerParams(
            collective_id=0, has_side_effects=True, vmem_limit_bytes=58 * 1024 * 1024
        ),
        cost_estimate=pl.CostEstimate(
            flops=10_000_000_000, bytes_accessed=4_000_000, transcendentals=262_144
        ),
    )(grad_out, saved_input, up_weight, down_weight, meta)


def solution(mesh):
    tokens = P(("dp", "expert"), None)
    return jax.shard_map(
        per_device,
        mesh=mesh,
        in_specs=(
            tokens, tokens, tokens, tokens,
            P("expert", "dp", None), P("expert", "dp", None),
            tokens, tokens, tokens,
        ),
        out_specs=(tokens, P(None, ("dp", "expert"), None)),
        check_vma=False,
    )
```

```python
import functools

import jax
import jax.numpy as jnp
from jax import lax
from jax.experimental import pallas as pl
from jax.experimental.pallas import tpu as pltpu
from jax.sharding import PartitionSpec as P

MESH = pl.DeviceIdType.MESH
F32 = jnp.float32
BF16 = jnp.bfloat16
NZ = 8
XL = 2
CORES = 2
FAR_Z = NZ // 2
XH = 2
NY = 4
NE = XH * NY
NX = XH * XL
PEERS = NY * CORES
EXPERTS = NE * CORES
TOK = 128
D = 2560
HID = 512
CAP = 32
HALF = D // 2
Q = 5
QW = HALF // Q
UPR = D // (XL * NZ * CORES)
DNR = HID // (XL * NZ * CORES)
BLOCKS = NZ * CORES
XROWS = PEERS * 2 * 16
TROWS = NX * XROWS
SET = PEERS * CAP


def mod(value, size):
    return lax.rem(value + size, size)


def nt_dot(a, b):
    return lax.dot_general(a, b, (((1,), (1,)), ((), ())), preferred_element_type=F32)


def kernel(
    grad_ref, input_ref, up_ref, down_ref, meta_ref,
    gi_ref, table_ref,
    up_buf, down_buf, far_x, far_g, far_meta, pick, far_pick, blend, far_blend,
    send_x, send_g, got_x, got_g, slope_buf, ret_send, ret_got, far_out, far_back,
    gbuf, mbuf, sel, dense, s1_got, s2_send, s2_got,
    pre_recv, pre_send, w_recv, w_send, x_recv, x2_recv, x_send, e_recv, e_send, m_recv, m_send, t_recv, t_send,
    f_recv, f_send, d_recv, d_send, r_recv, r_send, b_recv, b_send, s1_recv, s1_send, s2_recv, s2_send_sem,
):
    dp = lax.axis_index("dp")
    e = lax.axis_index("expert")
    c = lax.rem(dp, 2)
    z = lax.rem(dp // 2, NZ)
    xl = dp // (2 * NZ)
    xh, y = e // NY, lax.rem(e, NY)
    x = xh * 2 + xl
    oc, oxl = 1 - c, 1 - xl

    def dp_of(xl_, z_, c_):
        return (xl_ * NZ + z_) * 2 + c_

    def dev(x_, y_, z_, c_):
        return {"dp": dp_of(lax.rem(x_, 2), z_, c_), "expert": (x_ // 2) * NY + y_}

    sibling = dev(x, y, z, oc)
    ring = (dev(x, y, mod(z + 1, NZ), c), dev(x, y, mod(z - 1, NZ), c))
    across = dev(xh * 2 + 1 - xl, y, z, c)
    far = dev(NX - 1 - x, y, z, c)
    me8 = y * 2 + c
    near = [(1, 0), (3, 0), (2, 0), (1, 1), (3, 1), (2, 1), (0, 1)]

    def near_at(dy, dc):
        return lax.rem(y + dy, NY), (oc if dc else c)

    def remote(src, dst, send, recv, device):
        return pltpu.make_async_remote_copy(
            src_ref=src, dst_ref=dst, send_sem=send, recv_sem=recv,
            device_id=device, device_id_type=MESH,
        )

    barrier = pltpu.get_barrier_semaphore()
    friends = list(ring)
    for dx in range(1, NX):
        friends.append(dev(lax.rem(x + dx, NX), y, z, c))
    for dy, dc in near:
        y_, c_ = near_at(dy, dc)
        friends.append(dev(x, y_, z, c_))
    for friend in friends:
        pl.semaphore_signal(barrier, inc=1, device_id=friend, device_id_type=MESH)

    def up_rows(dp_, count):
        return pl.ds(pl.multiple_of(dp_ * UPR, 16), count)

    def down_rows(dp_, count):
        return pl.ds(pl.multiple_of(dp_ * DNR, 16), count)

    def tok_rows(block):
        return pl.ds(pl.multiple_of(block * TOK, TOK), TOK)

    def half_cols(order, q):
        return pl.ds(pl.multiple_of(order * HALF + q * QW, 128), QW)

    up_buf[up_rows(dp, UPR), :] = up_ref[c]
    down_buf[down_rows(dp, DNR), :] = down_ref[c]
    mine, theirs = z * 2 + c, z * 2 + oc
    mbuf[mine] = meta_ref[c]
    for q in range(Q):
        gbuf[q, tok_rows(mine), :] = grad_ref[:, half_cols(c, q)]

    numbers = lax.broadcasted_iota(jnp.int32, (EXPERTS, TOK), 0).astype(F32)
    zeros = jnp.zeros((EXPERTS, TOK), F32)
    earlier = jnp.where(
        lax.broadcasted_iota(jnp.int32, (TOK, TOK), 0)
        < lax.broadcasted_iota(jnp.int32, (TOK, TOK), 1),
        1.0, 0.0,
    ).astype(BF16)
    slots = lax.broadcasted_iota(jnp.int32, (CAP, TOK), 0).astype(F32)

    def choose(meta, pick_ref, blend_ref):
        hit0, hit1 = numbers == meta[0:1, :], numbers == meta[1:2, :]
        hits = jnp.where(hit0 | hit1, 1.0, 0.0)
        weight = jnp.where(hit0, meta[2:3, :], zeros) + jnp.where(hit1, meta[3:4, :], zeros)
        rank = jnp.dot(hits.astype(BF16), earlier, preferred_element_type=F32)
        place = jnp.where(hits > 0.5, rank, -1.0)
        for n in range(EXPERTS):
            chosen = slots == place[n : n + 1, :]
            rows = slice(n * CAP, (n + 1) * CAP)
            pick_ref[rows, :] = jnp.where(chosen, 1.0, 0.0).astype(BF16)
            blend_ref[rows, :] = jnp.where(chosen, weight[n : n + 1, :], 0.0)

    def dispatch(group, array):
        pick_ref = (pick, far_pick)[group]
        src = ((input_ref, grad_ref), (far_x, far_g))[group][array]
        out = (send_x, send_g)[array]
        onehot = pick_ref[pl.ds(pl.multiple_of(xh * SET, SET), SET), :]

        @pl.loop(0, 5)
        def _(n):
            cols = pl.ds(pl.multiple_of(n * 512, 512), 512)
            out[group * SET : (group + 1) * SET, cols] = jnp.dot(
                onehot, src[:, cols], preferred_element_type=F32
            ).astype(BF16)

    def slot_rows(group, m):
        return pl.ds(pl.multiple_of(group * SET + m * CAP, CAP), CAP)

    def dispatch_sends(group, array):
        out, got = ((send_x, got_x), (send_g, got_g))[array]
        for dy, dc in near:
            y_, c_ = near_at(dy, dc)
            remote(
                out.at[slot_rows(group, y_ * 2 + c_)], got.at[slot_rows(group, me8)],
                d_send.at[group, array], d_recv.at[group, array], dev(x, y_, z, c_),
            ).start()
        got[slot_rows(group, me8), :] = out[slot_rows(group, me8), :]

    choose(meta_ref[2], pick, blend)
    dispatch(0, 0)
    pl.semaphore_wait(barrier, len(friends))

    pre = [
        remote(up_ref.at[oc], up_buf.at[up_rows(dp, UPR)], pre_send.at[0], pre_recv.at[0], sibling),
        remote(
            down_ref.at[oc], down_buf.at[down_rows(dp, DNR)],
            pre_send.at[1], pre_recv.at[1], sibling,
        ),
        remote(meta_ref.at[oc], mbuf.at[mine], pre_send.at[2], pre_recv.at[2], sibling),
    ]
    for q in range(Q):
        pre.append(remote(
            grad_ref.at[:, half_cols(oc, q)], gbuf.at[q, tok_rows(mine)],
            pre_send.at[3 + q], pre_recv.at[3 + q], sibling,
        ))
    arrivals = [
        up_buf.at[up_rows(dp_of(xl, z, oc), UPR)],
        down_buf.at[down_rows(dp_of(xl, z, oc), DNR)],
        mbuf.at[theirs],
    ]
    for q in range(Q):
        arrivals.append(gbuf.at[q, tok_rows(theirs)])

    def pre_wait(at):
        remote(arrivals[at], arrivals[at], pre_send.at[at], pre_recv.at[at], sibling).wait_recv()

    def origin(d, s):
        return mod(z - s, NZ) if d == 0 else mod(z + s, NZ)

    def weight_rows(at, xl_, zs):
        dp_ = dp_of(xl_, zs, 0)
        if at == 0:
            return up_buf.at[up_rows(dp_, 2 * UPR)]
        return down_buf.at[down_rows(dp_, 2 * DNR)]

    def ring_parts(kind, d, s, half):
        zs = origin(d, s)
        if kind == "weights":
            return [
                (weight_rows(at, xl, zs), w_send.at[at], w_recv.at[d, at])
                for at in ((d,) if half else (0, 1))
            ]
        block, count = (zs * 2 + d, 1) if half else (zs * 2, 2)
        if kind == "meta":
            return [(mbuf.at[pl.ds(block, count)], m_send, m_recv.at[d])]
        rows = pl.ds(pl.multiple_of(block * TOK, TOK), count * TOK)
        return [(gbuf.at[kind, rows], t_send.at[kind], t_recv.at[d, kind])]

    def ring_send(kind, d, s):
        for block, send, recv in ring_parts(kind, d, s, s == FAR_Z - 1):
            remote(block, block, send, recv.at[s], ring[d]).start()

    def cross(block, at, recv):
        remote(block, block, x_send.at[at], recv, across).start()

    def ring_step(kind, s):
        for d in range(2):
            for block, send, recv in ring_parts(kind, d, s, s == FAR_Z):
                remote(block, block, send, recv.at[s - 1], ring[d]).wait_recv()
            if s < FAR_Z:
                ring_send(kind, d, s)
            if kind == "weights" and s != FAR_Z - 1:
                for at in (d,) if s == FAR_Z else (0, 1):
                    recv = x2_recv.at[at, d] if s == FAR_Z - 2 else x_recv.at[at]
                    cross(weight_rows(at, xl, origin(d, s)), at, recv)

    def wide_copy(d, at, s):
        block = weight_rows(at, oxl, origin(d, s))
        return remote(block, block, e_send.at[d, at], e_recv.at[d, at], ring[d])

    def wide_send(d):
        for at in range(2):
            block = weight_rows(at, oxl, origin(d, FAR_Z - 2))
            remote(block, block, x_send.at[at], x2_recv.at[at, d], across).wait_recv()
            wide_copy(d, at, FAR_Z - 2).start()

    def piece(q):
        pre_wait(3 + q)
        for d in range(2):
            ring_send(q, d, 0)

    def steps(*pairs):
        for kind, at in pairs:
            ring_step(kind, at)

    def far_copy(at):
        src, dst = ((input_ref, far_x), (meta_ref.at[2], far_meta), (grad_ref, far_g))[at]
        return remote(src, dst, f_send.at[at], f_recv.at[at], far)

    def set_out(at, block):
        for d in range(2):
            remote(block, block, w_send.at[at], w_recv.at[d, at, 0], ring[d]).start()
        cross(block, at, x_recv.at[at])

    for copy in pre[:4]:
        copy.start()
    for at in range(3):
        far_copy(at).start()
    set_out(0, up_buf.at[up_rows(dp, UPR)])
    set_out(1, down_buf.at[down_rows(dp, DNR)])
    dispatch_sends(0, 0)
    pre_wait(0)
    set_out(0, arrivals[0])
    pre_wait(1)
    set_out(1, arrivals[1])
    pre_wait(2)
    for d in range(2):
        ring_send("meta", d, 0)
    for copy in pre[4:]:
        copy.start()

    targets = (lax.broadcasted_iota(jnp.int32, (TROWS, TOK), 0) + z * TROWS).astype(F32)

    def select(block):
        cols = pl.ds(pl.multiple_of(block * TOK, TOK), TOK)
        meta = mbuf[block]
        one = jnp.where(targets == meta[1:2, :], meta[3:4, :], 0.0)
        sel[:, cols] = jnp.where(targets == meta[0:1, :], meta[2:3, :], one).astype(BF16)

    def all_bytes(ref, sem):
        pltpu.make_async_copy(ref, ref, sem).wait()

    def others(group):
        return pl.ds(group * SET, (PEERS - 1) * CAP)

    def expert_in(group):
        all_bytes(got_x.at[others(group)], d_recv.at[group, 0])
        all_bytes(got_g.at[others(group)], d_recv.at[group, 1])
        rows = pl.ds(group * SET, SET)

        @pl.loop(0, 2)
        def _(n):
            cols = pl.ds(pl.multiple_of(n * 256, 256), 256)
            before = jnp.dot(got_x[rows, :], up_buf[:, cols], preferred_element_type=F32)
            back = nt_dot(got_g[rows, :], down_buf[cols, :])
            sig = 1.0 / (1.0 + jnp.exp(-before))
            slope_buf[group, :, cols] = (back * sig * (1.0 + before * (1.0 - sig))).astype(BF16)

    def expert_out(group, part):
        rows = pl.ds(group * SET, SET)

        @pl.loop(part * 5, part * 5 + 5)
        def _(n):
            cols = pl.ds(pl.multiple_of(n * 256, 256), 256)
            ret_send[rows, cols] = nt_dot(slope_buf[group], up_buf[cols, :]).astype(BF16)

    def expert_send(group, part):
        cols = slice(part * HALF, (part + 1) * HALF)
        for dy, dc in near:
            y_, c_ = near_at(dy, dc)
            remote(
                ret_send.at[slot_rows(group, y_ * 2 + c_), cols],
                ret_got.at[slot_rows(group, me8), cols],
                r_send.at[group, part], r_recv.at[group, part], dev(x, y_, z, c_),
            ).start()
        ret_got[slot_rows(group, me8), cols] = ret_send[slot_rows(group, me8), cols]

    def returned(group, part):
        cols = pl.ds(part * HALF, HALF)
        all_bytes(ret_got.at[others(group), cols], r_recv.at[group, part])

    def mix_of(blend_ref):
        return blend_ref[pl.ds(pl.multiple_of(xh * SET, SET), SET), :].T.astype(BF16)

    def back_copy(part):
        cols = pl.ds(part * HALF, HALF)
        return remote(
            far_out.at[:, cols], far_back.at[:, cols], b_send.at[part], b_recv.at[part], far
        )

    def far_combine(part):
        returned(1, part)
        mix = mix_of(far_blend)

        @pl.loop(part * 5, part * 5 + 5)
        def _(n):
            cols = pl.ds(pl.multiple_of(n * 256, 256), 256)
            far_out[:, cols] = jnp.dot(
                mix, ret_got[SET : 2 * SET, cols], preferred_element_type=F32
            ).astype(BF16)

        back_copy(part).start()

    def x_rows(x_):
        return pl.ds(pl.multiple_of(x_ * XROWS, XROWS), XROWS)

    def m_rows(m):
        return pl.ds(pl.multiple_of(m * 32, 32), 32)

    def table_part(q):
        @pl.loop(0, TROWS // 256)
        def _(i):
            rows = pl.ds(pl.multiple_of(i * 256, 256), 256)
            dense[q, rows, :] = jnp.dot(
                sel[rows, :], gbuf[q], preferred_element_type=F32
            ).astype(BF16)

        for dx in (1, 3, 2):
            x_ = lax.rem(x + dx, NX)
            remote(
                dense.at[q, x_rows(x_)], s1_got.at[q, dx - 1],
                s1_send.at[q], s1_recv.at[q], dev(x_, y, z, c),
            ).start()

    def table_mid(q):
        all_bytes(s1_got.at[q], s1_recv.at[q])
        total = dense[q, x_rows(x), :].astype(F32)
        for k in range(NX - 1):
            total += s1_got[q, k].astype(F32)
        s2_send[q] = total.astype(BF16)
        for dy, dc in near:
            y_, c_ = near_at(dy, dc)
            remote(
                s2_send.at[q, m_rows(y_ * 2 + c_)], s2_got.at[q, c * NY + y],
                s2_send_sem.at[q], s2_recv.at[q], dev(x, y_, z, c_),
            ).start()
        s2_got[q, c * NY + y] = s2_send[q, m_rows(me8), :]

    def table_sum(q):
        all_bytes(s2_got.at[q, pl.ds(0, PEERS - 1)], s2_recv.at[q])
        for order in range(2):
            total = s2_got[q, order * NY].astype(F32)
            for k in range(1, NY):
                total += s2_got[q, order * NY + k].astype(F32)
            table_ref[order * 2 : order * 2 + 2, :, q * QW : (q + 1) * QW] = total.reshape(
                2, 16, QW
            )

    def sources(s):
        for d in range(2):
            for core in range(2) if s < FAR_Z else (d,):
                select(origin(d, s) * 2 + core)

    def far_inputs():
        far_copy(0).wait_recv()
        far_copy(1).wait_recv()
        choose(far_meta[...], far_pick, far_blend)
        dispatch(1, 0)
        dispatch_sends(1, 0)

    def far_grads():
        far_copy(2).wait_recv()
        dispatch(1, 1)
        dispatch_sends(1, 1)

    def own_grads():
        dispatch(0, 1)
        dispatch_sends(0, 1)

    def own_sources():
        select(mine)
        select(theirs)

    def weights_here():
        all_bytes(up_buf.at[pl.ds(0, 4 * 2 * UPR)], x_recv.at[0])
        all_bytes(down_buf.at[pl.ds(0, 4 * 2 * DNR)], x_recv.at[1])
        for d in range(2):
            for at in range(2):
                wide_copy(d, at, FAR_Z - 1).wait_recv()

    def combine(part):
        mix = mix_of(blend)
        returned(0, part)
        back_copy(part).wait_recv()

        @pl.loop(part * 5, part * 5 + 5)
        def _(n):
            cols = pl.ds(pl.multiple_of(n * 256, 256), 256)
            total = jnp.dot(mix, ret_got[0:SET, cols], preferred_element_type=F32)
            gi_ref[:, cols] = (total + far_back[:, cols].astype(F32)).astype(BF16)

    piece(0)
    own_grads()
    steps(("weights", 1), ("meta", 1))
    ring_step(0, 1)
    own_sources()
    sources(1)
    far_inputs()
    steps(("weights", 2), ("meta", 2))
    ring_step(0, 2)
    piece(1)
    piece(2)
    sources(2)
    far_grads()
    steps(("weights", 3), ("meta", 3))
    ring_step(0, 3)
    sources(3)
    steps(("weights", 4), ("meta", 4))
    wide_send(0)
    wide_send(1)
    sources(4)
    ring_step(0, 4)
    table_part(0)
    ring_step(1, 1)
    ring_step(2, 1)
    weights_here()
    expert_in(0)
    ring_step(1, 2)
    ring_step(2, 2)
    expert_out(0, 0)
    expert_send(0, 0)
    ring_step(1, 3)
    ring_step(2, 3)
    piece(3)
    piece(4)
    expert_out(0, 1)
    expert_in(1)
    expert_out(1, 0)
    expert_send(1, 0)
    ring_step(1, 4)
    expert_out(1, 1)
    expert_send(1, 1)
    expert_send(0, 1)
    ring_step(2, 4)
    ring_step(3, 1)
    ring_step(4, 1)
    table_part(1)
    table_mid(0)
    table_part(2)
    ring_step(3, 2)
    ring_step(4, 2)
    table_mid(1)
    ring_step(3, 3)
    ring_step(4, 3)
    far_combine(0)
    table_mid(2)
    ring_step(3, 4)
    table_part(3)
    ring_step(4, 4)
    table_part(4)
    far_combine(1)
    table_mid(3)
    table_mid(4)
    combine(0)
    combine(1)
    table_sum(0)
    table_sum(1)
    table_sum(2)
    table_sum(3)
    table_sum(4)

    for copy in pre:
        copy.wait_send()
    sends = 2 * (NZ - 1)
    all_bytes(up_buf.at[pl.ds(0, (NZ - 1) * 2 * UPR)], w_send.at[0])
    all_bytes(down_buf.at[pl.ds(0, (NZ - 1) * 2 * DNR)], w_send.at[1])
    all_bytes(up_buf.at[pl.ds(0, 6 * 2 * UPR)], x_send.at[0])
    all_bytes(down_buf.at[pl.ds(0, 6 * 2 * DNR)], x_send.at[1])
    for d in range(2):
        for at in range(2):
            wide_copy(d, at, FAR_Z - 2).wait_send()
    all_bytes(mbuf.at[pl.ds(0, sends)], m_send)
    for q in range(Q):
        all_bytes(gbuf.at[q, pl.ds(0, sends * TOK)], t_send.at[q])
        all_bytes(s1_got.at[q], s1_send.at[q])
        all_bytes(s2_got.at[q, pl.ds(0, PEERS - 1)], s2_send_sem.at[q])
    for at in range(3):
        far_copy(at).wait_send()
    for group in range(2):
        all_bytes(send_x.at[others(group)], d_send.at[group, 0])
        all_bytes(send_g.at[others(group)], d_send.at[group, 1])
        for part in range(2):
            all_bytes(ret_send.at[others(group), pl.ds(part * HALF, HALF)], r_send.at[group, part])
    for part in range(2):
        back_copy(part).wait_send()


def per_device(
    grad_out, saved_input, expert_ids, gate_weights, up_weight, down_weight,
    engram_gate, memory_owner, memory_slot,
):
    head = jnp.arange(4, dtype=jnp.int32)[None, :] % 2
    core = memory_owner % 2
    zs = (memory_owner // 2) % NZ
    xs = memory_owner // (2 * NZ)
    to = memory_slot // 16
    xs = (to // NY) * 2 + xs
    row = (((zs * NX + xs) * NY + to % NY) * 2 + core) * 32
    row = row + head * 16 + memory_slot % 16
    rows = jnp.concatenate([row, expert_ids], axis=1).astype(F32)
    gates = jnp.concatenate([engram_gate, gate_weights], axis=1)
    meta = jnp.concatenate(
        [
            rows.T.reshape(3, 2, TOK),
            gates.T.reshape(3, 2, TOK),
            jnp.zeros((3, 4, TOK), F32),
        ],
        axis=1,
    )

    vmem = pl.BlockSpec(memory_space=pltpu.VMEM)
    dma = pltpu.SemaphoreType.DMA
    return pl.pallas_call(
        kernel,
        out_shape=(
            jax.ShapeDtypeStruct((TOK, D), BF16),
            jax.ShapeDtypeStruct((4, 16, HALF), F32),
        ),
        in_specs=[vmem] * 5,
        out_specs=(vmem, vmem),
        scratch_shapes=[
            pltpu.VMEM((D, HID), BF16),
            pltpu.VMEM((HID, D), BF16),
            pltpu.VMEM((TOK, D), BF16),
            pltpu.VMEM((TOK, D), BF16),
            pltpu.VMEM((8, TOK), F32),
            pltpu.VMEM((EXPERTS * CAP, TOK), BF16),
            pltpu.VMEM((EXPERTS * CAP, TOK), BF16),
            pltpu.VMEM((EXPERTS * CAP, TOK), F32),
            pltpu.VMEM((EXPERTS * CAP, TOK), F32),
            pltpu.VMEM((EXPERTS * CAP, D), BF16),
            pltpu.VMEM((EXPERTS * CAP, D), BF16),
            pltpu.VMEM((EXPERTS * CAP, D), BF16),
            pltpu.VMEM((EXPERTS * CAP, D), BF16),
            pltpu.VMEM((2, SET, HID), BF16),
            pltpu.VMEM((EXPERTS * CAP, D), BF16),
            pltpu.VMEM((EXPERTS * CAP, D), BF16),
            pltpu.VMEM((TOK, D), BF16),
            pltpu.VMEM((TOK, D), BF16),
            pltpu.VMEM((Q, BLOCKS * TOK, QW), BF16),
            pltpu.VMEM((BLOCKS, 8, TOK), F32),
            pltpu.VMEM((TROWS, BLOCKS * TOK), BF16),
            pltpu.VMEM((Q, TROWS, QW), BF16),
            pltpu.VMEM((Q, NX - 1, XROWS, QW), BF16),
            pltpu.VMEM((Q, XROWS, QW), BF16),
            pltpu.VMEM((Q, PEERS, 32, QW), BF16),
            dma((3 + Q,)),
            dma((3 + Q,)),
            dma((2, 2, FAR_Z)),
            dma((2,)),
            dma((2,)),
            dma((2, 2)),
            dma((2,)),
            dma((2, 2)),
            dma((2, 2)),
            dma((2, FAR_Z)),
            dma(()),
            dma((2, Q, FAR_Z)),
            dma((Q,)),
            dma((3,)),
            dma((3,)),
            dma((2, 2)),
            dma((2, 2)),
            dma((2, 2)),
            dma((2, 2)),
            dma((2,)),
            dma((2,)),
            dma((Q,)),
            dma((Q,)),
            dma((Q,)),
            dma((Q,)),
        ],
        compiler_params=pltpu.CompilerParams(
            collective_id=0, has_side_effects=True, vmem_limit_bytes=58 * 1024 * 1024
        ),
        cost_estimate=pl.CostEstimate(
            flops=10_000_000_000, bytes_accessed=4_000_000, transcendentals=262_144
        ),
    )(grad_out, saved_input, up_weight, down_weight, meta)


def solution(mesh):
    tokens = P(("dp", "expert"), None)
    return jax.shard_map(
        per_device,
        mesh=mesh,
        in_specs=(
            tokens, tokens, tokens, tokens,
            P("expert", "dp", None), P("expert", "dp", None),
            tokens, tokens, tokens,
        ),
        out_specs=(tokens, P(None, ("dp", "expert"), None)),
        check_vma=False,
    )
```

```python
import functools

import jax
import jax.numpy as jnp
from jax import lax
from jax.experimental import pallas as pl
from jax.experimental.pallas import tpu as pltpu
from jax.sharding import PartitionSpec as P

MESH = pl.DeviceIdType.MESH
F32 = jnp.float32
BF16 = jnp.bfloat16
NZ = 8
XL = 2
CORES = 2
FAR_Z = NZ // 2
XH = 2
NY = 4
NE = XH * NY
NX = XH * XL
PEERS = NY * CORES
EXPERTS = NE * CORES
TOK = 128
D = 2560
HID = 512
CAP = 32
HALF = D // 2
Q = 5
QW = HALF // Q
UPR = D // (XL * NZ * CORES)
DNR = HID // (XL * NZ * CORES)
BLOCKS = NZ * CORES
XROWS = PEERS * 2 * 16
TROWS = NX * XROWS
SET = PEERS * CAP


def mod(value, size):
    return lax.rem(value + size, size)


def nt_dot(a, b):
    return lax.dot_general(a, b, (((1,), (1,)), ((), ())), preferred_element_type=F32)


def kernel(
    grad_ref, input_ref, up_ref, down_ref, meta_ref,
    gi_ref, table_ref,
    up_buf, down_buf, far_x, far_g, far_meta, pick, far_pick, blend, far_blend,
    send_x, send_g, got_x, got_g, slope_buf, ret_send, ret_got, far_out, far_back,
    gbuf, mbuf, sel, dense, s1_got, s2_send, s2_got,
    pre_recv, pre_send, w_recv, w_send, x_recv, x2_recv, x_send, e_recv, e_send, m_recv, m_send, t_recv, t_send,
    f_recv, f_send, d_recv, d_send, r_recv, r_send, b_recv, b_send, s1_recv, s1_send, s2_recv, s2_send_sem,
):
    dp = lax.axis_index("dp")
    e = lax.axis_index("expert")
    c = lax.rem(dp, 2)
    z = lax.rem(dp // 2, NZ)
    xl = dp // (2 * NZ)
    xh, y = e // NY, lax.rem(e, NY)
    x = xh * 2 + xl
    oc, oxl = 1 - c, 1 - xl

    def dp_of(xl_, z_, c_):
        return (xl_ * NZ + z_) * 2 + c_

    def dev(x_, y_, z_, c_):
        return {"dp": dp_of(lax.rem(x_, 2), z_, c_), "expert": (x_ // 2) * NY + y_}

    sibling = dev(x, y, z, oc)
    ring = (dev(x, y, mod(z + 1, NZ), c), dev(x, y, mod(z - 1, NZ), c))
    across = dev(xh * 2 + 1 - xl, y, z, c)
    far = dev(NX - 1 - x, y, z, c)
    me8 = y * 2 + c
    near = [(1, 0), (3, 0), (2, 0), (1, 1), (3, 1), (2, 1), (0, 1)]

    def near_at(dy, dc):
        return lax.rem(y + dy, NY), (oc if dc else c)

    def remote(src, dst, send, recv, device):
        return pltpu.make_async_remote_copy(
            src_ref=src, dst_ref=dst, send_sem=send, recv_sem=recv,
            device_id=device, device_id_type=MESH,
        )

    barrier = pltpu.get_barrier_semaphore()
    friends = list(ring)
    for dx in range(1, NX):
        friends.append(dev(lax.rem(x + dx, NX), y, z, c))
    for dy, dc in near:
        y_, c_ = near_at(dy, dc)
        friends.append(dev(x, y_, z, c_))
    for friend in friends:
        pl.semaphore_signal(barrier, inc=1, device_id=friend, device_id_type=MESH)

    def up_rows(dp_, count):
        return pl.ds(pl.multiple_of(dp_ * UPR, 16), count)

    def down_rows(dp_, count):
        return pl.ds(pl.multiple_of(dp_ * DNR, 16), count)

    def tok_rows(block):
        return pl.ds(pl.multiple_of(block * TOK, TOK), TOK)

    def half_cols(order, q):
        return pl.ds(pl.multiple_of(order * HALF + q * QW, 128), QW)

    up_buf[up_rows(dp, UPR), :] = up_ref[c]
    down_buf[down_rows(dp, DNR), :] = down_ref[c]
    mine, theirs = z * 2 + c, z * 2 + oc
    mbuf[mine] = meta_ref[c]
    for q in range(Q):
        gbuf[q, tok_rows(mine), :] = grad_ref[:, half_cols(c, q)]

    numbers = lax.broadcasted_iota(jnp.int32, (EXPERTS, TOK), 0).astype(F32)
    zeros = jnp.zeros((EXPERTS, TOK), F32)
    earlier = jnp.where(
        lax.broadcasted_iota(jnp.int32, (TOK, TOK), 0)
        < lax.broadcasted_iota(jnp.int32, (TOK, TOK), 1),
        1.0, 0.0,
    ).astype(BF16)
    slots = lax.broadcasted_iota(jnp.int32, (CAP, TOK), 0).astype(F32)

    def choose(meta, pick_ref, blend_ref):
        hit0, hit1 = numbers == meta[0:1, :], numbers == meta[1:2, :]
        hits = jnp.where(hit0 | hit1, 1.0, 0.0)
        weight = jnp.where(hit0, meta[2:3, :], zeros) + jnp.where(hit1, meta[3:4, :], zeros)
        rank = jnp.dot(hits.astype(BF16), earlier, preferred_element_type=F32)
        place = jnp.where(hits > 0.5, rank, -1.0)
        for n in range(EXPERTS):
            chosen = slots == place[n : n + 1, :]
            rows = slice(n * CAP, (n + 1) * CAP)
            pick_ref[rows, :] = jnp.where(chosen, 1.0, 0.0).astype(BF16)
            blend_ref[rows, :] = jnp.where(chosen, weight[n : n + 1, :], 0.0)

    def dispatch(group, array):
        pick_ref = (pick, far_pick)[group]
        src = ((input_ref, grad_ref), (far_x, far_g))[group][array]
        out = (send_x, send_g)[array]
        onehot = pick_ref[pl.ds(pl.multiple_of(xh * SET, SET), SET), :]

        @pl.loop(0, 5)
        def _(n):
            cols = pl.ds(pl.multiple_of(n * 512, 512), 512)
            out[group * SET : (group + 1) * SET, cols] = jnp.dot(
                onehot, src[:, cols], preferred_element_type=F32
            ).astype(BF16)

    def slot_rows(group, m):
        return pl.ds(pl.multiple_of(group * SET + m * CAP, CAP), CAP)

    def dispatch_sends(group, array):
        out, got = ((send_x, got_x), (send_g, got_g))[array]
        for dy, dc in near:
            y_, c_ = near_at(dy, dc)
            remote(
                out.at[slot_rows(group, y_ * 2 + c_)], got.at[slot_rows(group, me8)],
                d_send.at[group, array], d_recv.at[group, array], dev(x, y_, z, c_),
            ).start()
        got[slot_rows(group, me8), :] = out[slot_rows(group, me8), :]

    choose(meta_ref[2], pick, blend)
    dispatch(0, 0)
    pl.semaphore_wait(barrier, len(friends))

    pre = [
        remote(up_ref.at[oc], up_buf.at[up_rows(dp, UPR)], pre_send.at[0], pre_recv.at[0], sibling),
        remote(
            down_ref.at[oc], down_buf.at[down_rows(dp, DNR)],
            pre_send.at[1], pre_recv.at[1], sibling,
        ),
        remote(meta_ref.at[oc], mbuf.at[mine], pre_send.at[2], pre_recv.at[2], sibling),
    ]
    for q in range(Q):
        pre.append(remote(
            grad_ref.at[:, half_cols(oc, q)], gbuf.at[q, tok_rows(mine)],
            pre_send.at[3 + q], pre_recv.at[3 + q], sibling,
        ))
    arrivals = [
        up_buf.at[up_rows(dp_of(xl, z, oc), UPR)],
        down_buf.at[down_rows(dp_of(xl, z, oc), DNR)],
        mbuf.at[theirs],
    ]
    for q in range(Q):
        arrivals.append(gbuf.at[q, tok_rows(theirs)])

    def pre_wait(at):
        remote(arrivals[at], arrivals[at], pre_send.at[at], pre_recv.at[at], sibling).wait_recv()

    def origin(d, s):
        return mod(z - s, NZ) if d == 0 else mod(z + s, NZ)

    def weight_rows(at, xl_, zs):
        dp_ = dp_of(xl_, zs, 0)
        if at == 0:
            return up_buf.at[up_rows(dp_, 2 * UPR)]
        return down_buf.at[down_rows(dp_, 2 * DNR)]

    def ring_parts(kind, d, s, half):
        zs = origin(d, s)
        if kind == "weights":
            return [
                (weight_rows(at, xl, zs), w_send.at[at], w_recv.at[d, at])
                for at in ((d,) if half else (0, 1))
            ]
        block, count = (zs * 2 + d, 1) if half else (zs * 2, 2)
        if kind == "meta":
            return [(mbuf.at[pl.ds(block, count)], m_send, m_recv.at[d])]
        rows = pl.ds(pl.multiple_of(block * TOK, TOK), count * TOK)
        return [(gbuf.at[kind, rows], t_send.at[kind], t_recv.at[d, kind])]

    def ring_send(kind, d, s):
        for block, send, recv in ring_parts(kind, d, s, s == FAR_Z - 1):
            remote(block, block, send, recv.at[s], ring[d]).start()

    def cross(block, at, recv):
        remote(block, block, x_send.at[at], recv, across).start()

    def ring_step(kind, s):
        for d in range(2):
            for block, send, recv in ring_parts(kind, d, s, s == FAR_Z):
                remote(block, block, send, recv.at[s - 1], ring[d]).wait_recv()
            if s < FAR_Z:
                ring_send(kind, d, s)
            if kind == "weights" and s != FAR_Z - 1:
                for at in (d,) if s == FAR_Z else (0, 1):
                    recv = x2_recv.at[at, d] if s == FAR_Z - 2 else x_recv.at[at]
                    cross(weight_rows(at, xl, origin(d, s)), at, recv)

    def wide_copy(d, at, s):
        block = weight_rows(at, oxl, origin(d, s))
        return remote(block, block, e_send.at[d, at], e_recv.at[d, at], ring[d])

    def wide_send(d):
        for at in range(2):
            block = weight_rows(at, oxl, origin(d, FAR_Z - 2))
            remote(block, block, x_send.at[at], x2_recv.at[at, d], across).wait_recv()
            wide_copy(d, at, FAR_Z - 2).start()

    def piece(q):
        pre_wait(3 + q)
        for d in range(2):
            ring_send(q, d, 0)

    def steps(*pairs):
        for kind, at in pairs:
            ring_step(kind, at)

    def far_copy(at):
        src, dst = ((input_ref, far_x), (meta_ref.at[2], far_meta), (grad_ref, far_g))[at]
        return remote(src, dst, f_send.at[at], f_recv.at[at], far)

    def set_out(at, block):
        for d in range(2):
            remote(block, block, w_send.at[at], w_recv.at[d, at, 0], ring[d]).start()
        cross(block, at, x_recv.at[at])

    for copy in pre[:4]:
        copy.start()
    for at in range(3):
        far_copy(at).start()
    set_out(0, up_buf.at[up_rows(dp, UPR)])
    set_out(1, down_buf.at[down_rows(dp, DNR)])
    dispatch_sends(0, 0)
    pre_wait(0)
    set_out(0, arrivals[0])
    pre_wait(1)
    set_out(1, arrivals[1])
    pre_wait(2)
    for d in range(2):
        ring_send("meta", d, 0)
    for copy in pre[4:]:
        copy.start()

    targets = (lax.broadcasted_iota(jnp.int32, (TROWS, TOK), 0) + z * TROWS).astype(F32)

    def select(block):
        cols = pl.ds(pl.multiple_of(block * TOK, TOK), TOK)
        meta = mbuf[block]
        one = jnp.where(targets == meta[1:2, :], meta[3:4, :], 0.0)
        sel[:, cols] = jnp.where(targets == meta[0:1, :], meta[2:3, :], one).astype(BF16)

    def all_bytes(ref, sem):
        pltpu.make_async_copy(ref, ref, sem).wait()

    def others(group):
        return pl.ds(group * SET, (PEERS - 1) * CAP)

    def expert_in(group):
        all_bytes(got_x.at[others(group)], d_recv.at[group, 0])
        all_bytes(got_g.at[others(group)], d_recv.at[group, 1])
        rows = pl.ds(group * SET, SET)

        @pl.loop(0, 2)
        def _(n):
            cols = pl.ds(pl.multiple_of(n * 256, 256), 256)
            before = jnp.dot(got_x[rows, :], up_buf[:, cols], preferred_element_type=F32)
            back = nt_dot(got_g[rows, :], down_buf[cols, :])
            sig = 1.0 / (1.0 + jnp.exp(-before))
            slope_buf[group, :, cols] = (back * sig * (1.0 + before * (1.0 - sig))).astype(BF16)

    def expert_out(group, part):
        rows = pl.ds(group * SET, SET)

        @pl.loop(part * 5, part * 5 + 5)
        def _(n):
            cols = pl.ds(pl.multiple_of(n * 256, 256), 256)
            ret_send[rows, cols] = nt_dot(slope_buf[group], up_buf[cols, :]).astype(BF16)

    def expert_send(group, part):
        cols = slice(part * HALF, (part + 1) * HALF)
        for dy, dc in near:
            y_, c_ = near_at(dy, dc)
            remote(
                ret_send.at[slot_rows(group, y_ * 2 + c_), cols],
                ret_got.at[slot_rows(group, me8), cols],
                r_send.at[group, part], r_recv.at[group, part], dev(x, y_, z, c_),
            ).start()
        ret_got[slot_rows(group, me8), cols] = ret_send[slot_rows(group, me8), cols]

    def returned(group, part):
        cols = pl.ds(part * HALF, HALF)
        all_bytes(ret_got.at[others(group), cols], r_recv.at[group, part])

    def mix_of(blend_ref):
        return blend_ref[pl.ds(pl.multiple_of(xh * SET, SET), SET), :].T.astype(BF16)

    def back_copy(part):
        cols = pl.ds(part * HALF, HALF)
        return remote(
            far_out.at[:, cols], far_back.at[:, cols], b_send.at[part], b_recv.at[part], far
        )

    def far_combine(part):
        returned(1, part)
        mix = mix_of(far_blend)

        @pl.loop(part * 5, part * 5 + 5)
        def _(n):
            cols = pl.ds(pl.multiple_of(n * 256, 256), 256)
            far_out[:, cols] = jnp.dot(
                mix, ret_got[SET : 2 * SET, cols], preferred_element_type=F32
            ).astype(BF16)

        back_copy(part).start()

    def x_rows(x_):
        return pl.ds(pl.multiple_of(x_ * XROWS, XROWS), XROWS)

    def m_rows(m):
        return pl.ds(pl.multiple_of(m * 32, 32), 32)

    def table_part(q):
        @pl.loop(0, TROWS // 256)
        def _(i):
            rows = pl.ds(pl.multiple_of(i * 256, 256), 256)
            dense[q, rows, :] = jnp.dot(
                sel[rows, :], gbuf[q], preferred_element_type=F32
            ).astype(BF16)

        for dx in (1, 3, 2):
            x_ = lax.rem(x + dx, NX)
            remote(
                dense.at[q, x_rows(x_)], s1_got.at[q, dx - 1],
                s1_send.at[q], s1_recv.at[q], dev(x_, y, z, c),
            ).start()

    def table_mid(q):
        all_bytes(s1_got.at[q], s1_recv.at[q])
        total = dense[q, x_rows(x), :].astype(F32)
        for k in range(NX - 1):
            total += s1_got[q, k].astype(F32)
        s2_send[q] = total.astype(BF16)
        for dy, dc in near:
            y_, c_ = near_at(dy, dc)
            remote(
                s2_send.at[q, m_rows(y_ * 2 + c_)], s2_got.at[q, c * NY + y],
                s2_send_sem.at[q], s2_recv.at[q], dev(x, y_, z, c_),
            ).start()
        s2_got[q, c * NY + y] = s2_send[q, m_rows(me8), :]

    def table_sum(q):
        all_bytes(s2_got.at[q, pl.ds(0, PEERS - 1)], s2_recv.at[q])
        for order in range(2):
            total = s2_got[q, order * NY].astype(F32)
            for k in range(1, NY):
                total += s2_got[q, order * NY + k].astype(F32)
            table_ref[order * 2 : order * 2 + 2, :, q * QW : (q + 1) * QW] = total.reshape(
                2, 16, QW
            )

    def sources(s):
        for d in range(2):
            for core in range(2) if s < FAR_Z else (d,):
                select(origin(d, s) * 2 + core)

    def far_inputs():
        far_copy(0).wait_recv()
        far_copy(1).wait_recv()
        choose(far_meta[...], far_pick, far_blend)
        dispatch(1, 0)
        dispatch_sends(1, 0)

    def far_grads():
        far_copy(2).wait_recv()
        dispatch(1, 1)
        dispatch_sends(1, 1)

    def own_grads():
        dispatch(0, 1)
        dispatch_sends(0, 1)

    def own_sources():
        select(mine)
        select(theirs)

    def weights_here():
        all_bytes(up_buf.at[pl.ds(0, 4 * 2 * UPR)], x_recv.at[0])
        all_bytes(down_buf.at[pl.ds(0, 4 * 2 * DNR)], x_recv.at[1])
        for d in range(2):
            for at in range(2):
                wide_copy(d, at, FAR_Z - 1).wait_recv()

    def combine(part):
        mix = mix_of(blend)
        returned(0, part)
        back_copy(part).wait_recv()

        @pl.loop(part * 5, part * 5 + 5)
        def _(n):
            cols = pl.ds(pl.multiple_of(n * 256, 256), 256)
            total = jnp.dot(mix, ret_got[0:SET, cols], preferred_element_type=F32)
            gi_ref[:, cols] = (total + far_back[:, cols].astype(F32)).astype(BF16)

    piece(0)
    own_grads()
    steps(("weights", 1), ("meta", 1))
    ring_step(0, 1)
    own_sources()
    sources(1)
    far_inputs()
    steps(("weights", 2), ("meta", 2))
    ring_step(0, 2)
    piece(1)
    piece(2)
    sources(2)
    far_grads()
    steps(("weights", 3), ("meta", 3))
    ring_step(0, 3)
    sources(3)
    steps(("weights", 4), ("meta", 4))
    wide_send(0)
    wide_send(1)
    sources(4)
    ring_step(0, 4)
    table_part(0)
    ring_step(1, 1)
    ring_step(2, 1)
    weights_here()
    expert_in(0)
    ring_step(1, 2)
    ring_step(2, 2)
    expert_out(0, 0)
    expert_send(0, 0)
    ring_step(1, 3)
    ring_step(2, 3)
    piece(3)
    piece(4)
    expert_in(1)
    expert_out(1, 0)
    expert_send(1, 0)
    ring_step(1, 4)
    expert_out(1, 1)
    expert_send(1, 1)
    expert_out(0, 1)
    expert_send(0, 1)
    ring_step(2, 4)
    ring_step(3, 1)
    ring_step(4, 1)
    table_part(1)
    table_mid(0)
    table_part(2)
    ring_step(3, 2)
    ring_step(4, 2)
    table_mid(1)
    ring_step(3, 3)
    ring_step(4, 3)
    far_combine(0)
    table_mid(2)
    ring_step(3, 4)
    table_part(3)
    ring_step(4, 4)
    table_part(4)
    far_combine(1)
    table_sum(0)
    table_sum(1)
    table_sum(2)
    table_mid(3)
    combine(0)
    table_mid(4)
    combine(1)
    table_sum(3)
    table_sum(4)

    for copy in pre:
        copy.wait_send()
    sends = 2 * (NZ - 1)
    all_bytes(up_buf.at[pl.ds(0, (NZ - 1) * 2 * UPR)], w_send.at[0])
    all_bytes(down_buf.at[pl.ds(0, (NZ - 1) * 2 * DNR)], w_send.at[1])
    all_bytes(up_buf.at[pl.ds(0, 6 * 2 * UPR)], x_send.at[0])
    all_bytes(down_buf.at[pl.ds(0, 6 * 2 * DNR)], x_send.at[1])
    for d in range(2):
        for at in range(2):
            wide_copy(d, at, FAR_Z - 2).wait_send()
    all_bytes(mbuf.at[pl.ds(0, sends)], m_send)
    for q in range(Q):
        all_bytes(gbuf.at[q, pl.ds(0, sends * TOK)], t_send.at[q])
        all_bytes(s1_got.at[q], s1_send.at[q])
        all_bytes(s2_got.at[q, pl.ds(0, PEERS - 1)], s2_send_sem.at[q])
    for at in range(3):
        far_copy(at).wait_send()
    for group in range(2):
        all_bytes(send_x.at[others(group)], d_send.at[group, 0])
        all_bytes(send_g.at[others(group)], d_send.at[group, 1])
        for part in range(2):
            all_bytes(ret_send.at[others(group), pl.ds(part * HALF, HALF)], r_send.at[group, part])
    for part in range(2):
        back_copy(part).wait_send()


def per_device(
    grad_out, saved_input, expert_ids, gate_weights, up_weight, down_weight,
    engram_gate, memory_owner, memory_slot,
):
    head = jnp.arange(4, dtype=jnp.int32)[None, :] % 2
    core = memory_owner % 2
    zs = (memory_owner // 2) % NZ
    xs = memory_owner // (2 * NZ)
    to = memory_slot // 16
    xs = (to // NY) * 2 + xs
    row = (((zs * NX + xs) * NY + to % NY) * 2 + core) * 32
    row = row + head * 16 + memory_slot % 16
    rows = jnp.concatenate([row, expert_ids], axis=1).astype(F32)
    gates = jnp.concatenate([engram_gate, gate_weights], axis=1)
    meta = jnp.concatenate(
        [
            rows.T.reshape(3, 2, TOK),
            gates.T.reshape(3, 2, TOK),
            jnp.zeros((3, 4, TOK), F32),
        ],
        axis=1,
    )

    vmem = pl.BlockSpec(memory_space=pltpu.VMEM)
    dma = pltpu.SemaphoreType.DMA
    return pl.pallas_call(
        kernel,
        out_shape=(
            jax.ShapeDtypeStruct((TOK, D), BF16),
            jax.ShapeDtypeStruct((4, 16, HALF), F32),
        ),
        in_specs=[vmem] * 5,
        out_specs=(vmem, vmem),
        scratch_shapes=[
            pltpu.VMEM((D, HID), BF16),
            pltpu.VMEM((HID, D), BF16),
            pltpu.VMEM((TOK, D), BF16),
            pltpu.VMEM((TOK, D), BF16),
            pltpu.VMEM((8, TOK), F32),
            pltpu.VMEM((EXPERTS * CAP, TOK), BF16),
            pltpu.VMEM((EXPERTS * CAP, TOK), BF16),
            pltpu.VMEM((EXPERTS * CAP, TOK), F32),
            pltpu.VMEM((EXPERTS * CAP, TOK), F32),
            pltpu.VMEM((EXPERTS * CAP, D), BF16),
            pltpu.VMEM((EXPERTS * CAP, D), BF16),
            pltpu.VMEM((EXPERTS * CAP, D), BF16),
            pltpu.VMEM((EXPERTS * CAP, D), BF16),
            pltpu.VMEM((2, SET, HID), BF16),
            pltpu.VMEM((EXPERTS * CAP, D), BF16),
            pltpu.VMEM((EXPERTS * CAP, D), BF16),
            pltpu.VMEM((TOK, D), BF16),
            pltpu.VMEM((TOK, D), BF16),
            pltpu.VMEM((Q, BLOCKS * TOK, QW), BF16),
            pltpu.VMEM((BLOCKS, 8, TOK), F32),
            pltpu.VMEM((TROWS, BLOCKS * TOK), BF16),
            pltpu.VMEM((Q, TROWS, QW), BF16),
            pltpu.VMEM((Q, NX - 1, XROWS, QW), BF16),
            pltpu.VMEM((Q, XROWS, QW), BF16),
            pltpu.VMEM((Q, PEERS, 32, QW), BF16),
            dma((3 + Q,)),
            dma((3 + Q,)),
            dma((2, 2, FAR_Z)),
            dma((2,)),
            dma((2,)),
            dma((2, 2)),
            dma((2,)),
            dma((2, 2)),
            dma((2, 2)),
            dma((2, FAR_Z)),
            dma(()),
            dma((2, Q, FAR_Z)),
            dma((Q,)),
            dma((3,)),
            dma((3,)),
            dma((2, 2)),
            dma((2, 2)),
            dma((2, 2)),
            dma((2, 2)),
            dma((2,)),
            dma((2,)),
            dma((Q,)),
            dma((Q,)),
            dma((Q,)),
            dma((Q,)),
        ],
        compiler_params=pltpu.CompilerParams(
            collective_id=0, has_side_effects=True, vmem_limit_bytes=58 * 1024 * 1024
        ),
        cost_estimate=pl.CostEstimate(
            flops=10_000_000_000, bytes_accessed=4_000_000, transcendentals=262_144
        ),
    )(grad_out, saved_input, up_weight, down_weight, meta)


def solution(mesh):
    tokens = P(("dp", "expert"), None)
    return jax.shard_map(
        per_device,
        mesh=mesh,
        in_specs=(
            tokens, tokens, tokens, tokens,
            P("expert", "dp", None), P("expert", "dp", None),
            tokens, tokens, tokens,
        ),
        out_specs=(tokens, P(None, ("dp", "expert"), None)),
        check_vma=False,
    )
```

```python
import functools

import jax
import jax.numpy as jnp
from jax import lax
from jax.experimental import pallas as pl
from jax.experimental.pallas import tpu as pltpu
from jax.sharding import PartitionSpec as P

MESH = pl.DeviceIdType.MESH
F32 = jnp.float32
BF16 = jnp.bfloat16
NZ = 8
XL = 2
CORES = 2
FAR_Z = NZ // 2
XH = 2
NY = 4
NE = XH * NY
NX = XH * XL
PEERS = NY * CORES
EXPERTS = NE * CORES
TOK = 128
D = 2560
HID = 512
CAP = 32
HALF = D // 2
Q = 5
QW = HALF // Q
UPR = D // (XL * NZ * CORES)
DNR = HID // (XL * NZ * CORES)
BLOCKS = NZ * CORES
XROWS = PEERS * 2 * 16
TROWS = NX * XROWS
SET = PEERS * CAP


def mod(value, size):
    return lax.rem(value + size, size)


def nt_dot(a, b):
    return lax.dot_general(a, b, (((1,), (1,)), ((), ())), preferred_element_type=F32)


def kernel(
    grad_ref, input_ref, up_ref, down_ref, meta_ref,
    gi_ref, table_ref,
    up_buf, down_buf, far_x, far_g, far_meta, pick, far_pick, blend, far_blend,
    send_x, send_g, got_x, got_g, pre_buf, slope_buf, ret_send, ret_got, far_out, far_back,
    gbuf, mbuf, sel, dense, s1_got, s2_send, s2_got,
    pre_recv, pre_send, w_recv, w_send, x_recv, x2_recv, x_send, e_recv, e_send, m_recv, m_send, t_recv, t_send,
    f_recv, f_send, d_recv, d_send, r_recv, r_send, b_recv, b_send, s1_recv, s1_send, s2_recv, s2_send_sem,
):
    dp = lax.axis_index("dp")
    e = lax.axis_index("expert")
    c = lax.rem(dp, 2)
    z = lax.rem(dp // 2, NZ)
    xl = dp // (2 * NZ)
    xh, y = e // NY, lax.rem(e, NY)
    x = xh * 2 + xl
    oc, oxl = 1 - c, 1 - xl

    def dp_of(xl_, z_, c_):
        return (xl_ * NZ + z_) * 2 + c_

    def dev(x_, y_, z_, c_):
        return {"dp": dp_of(lax.rem(x_, 2), z_, c_), "expert": (x_ // 2) * NY + y_}

    sibling = dev(x, y, z, oc)
    ring = (dev(x, y, mod(z + 1, NZ), c), dev(x, y, mod(z - 1, NZ), c))
    across = dev(xh * 2 + 1 - xl, y, z, c)
    far = dev(NX - 1 - x, y, z, c)
    me8 = y * 2 + c
    near = [(1, 0), (3, 0), (2, 0), (1, 1), (3, 1), (2, 1), (0, 1)]

    def near_at(dy, dc):
        return lax.rem(y + dy, NY), (oc if dc else c)

    def remote(src, dst, send, recv, device):
        return pltpu.make_async_remote_copy(
            src_ref=src, dst_ref=dst, send_sem=send, recv_sem=recv,
            device_id=device, device_id_type=MESH,
        )

    barrier = pltpu.get_barrier_semaphore()
    friends = list(ring)
    for dx in range(1, NX):
        friends.append(dev(lax.rem(x + dx, NX), y, z, c))
    for dy, dc in near:
        y_, c_ = near_at(dy, dc)
        friends.append(dev(x, y_, z, c_))
    for friend in friends:
        pl.semaphore_signal(barrier, inc=1, device_id=friend, device_id_type=MESH)

    def up_rows(dp_, count):
        return pl.ds(pl.multiple_of(dp_ * UPR, 16), count)

    def down_rows(dp_, count):
        return pl.ds(pl.multiple_of(dp_ * DNR, 16), count)

    def tok_rows(block):
        return pl.ds(pl.multiple_of(block * TOK, TOK), TOK)

    def half_cols(order, q):
        return pl.ds(pl.multiple_of(order * HALF + q * QW, 128), QW)

    up_buf[up_rows(dp, UPR), :] = up_ref[c]
    down_buf[down_rows(dp, DNR), :] = down_ref[c]
    mine, theirs = z * 2 + c, z * 2 + oc
    mbuf[mine] = meta_ref[c]
    for q in range(Q):
        gbuf[q, tok_rows(mine), :] = grad_ref[:, half_cols(c, q)]

    numbers = lax.broadcasted_iota(jnp.int32, (EXPERTS, TOK), 0).astype(F32)
    zeros = jnp.zeros((EXPERTS, TOK), F32)
    earlier = jnp.where(
        lax.broadcasted_iota(jnp.int32, (TOK, TOK), 0)
        < lax.broadcasted_iota(jnp.int32, (TOK, TOK), 1),
        1.0, 0.0,
    ).astype(BF16)
    slots = lax.broadcasted_iota(jnp.int32, (CAP, TOK), 0).astype(F32)

    def choose(meta, pick_ref, blend_ref):
        hit0, hit1 = numbers == meta[0:1, :], numbers == meta[1:2, :]
        hits = jnp.where(hit0 | hit1, 1.0, 0.0)
        weight = jnp.where(hit0, meta[2:3, :], zeros) + jnp.where(hit1, meta[3:4, :], zeros)
        rank = jnp.dot(hits.astype(BF16), earlier, preferred_element_type=F32)
        place = jnp.where(hits > 0.5, rank, -1.0)
        for n in range(EXPERTS):
            chosen = slots == place[n : n + 1, :]
            rows = slice(n * CAP, (n + 1) * CAP)
            pick_ref[rows, :] = jnp.where(chosen, 1.0, 0.0).astype(BF16)
            blend_ref[rows, :] = jnp.where(chosen, weight[n : n + 1, :], 0.0)

    def dispatch(group, array):
        pick_ref = (pick, far_pick)[group]
        src = ((input_ref, grad_ref), (far_x, far_g))[group][array]
        out = (send_x, send_g)[array]
        onehot = pick_ref[pl.ds(pl.multiple_of(xh * SET, SET), SET), :]

        @pl.loop(0, 5)
        def _(n):
            cols = pl.ds(pl.multiple_of(n * 512, 512), 512)
            out[group * SET : (group + 1) * SET, cols] = jnp.dot(
                onehot, src[:, cols], preferred_element_type=F32
            ).astype(BF16)

    def slot_rows(group, m):
        return pl.ds(pl.multiple_of(group * SET + m * CAP, CAP), CAP)

    def dispatch_sends(group, array):
        out, got = ((send_x, got_x), (send_g, got_g))[array]
        for dy, dc in near:
            y_, c_ = near_at(dy, dc)
            remote(
                out.at[slot_rows(group, y_ * 2 + c_)], got.at[slot_rows(group, me8)],
                d_send.at[group, array], d_recv.at[group, array], dev(x, y_, z, c_),
            ).start()
        got[slot_rows(group, me8), :] = out[slot_rows(group, me8), :]

    choose(meta_ref[2], pick, blend)
    dispatch(0, 0)
    pl.semaphore_wait(barrier, len(friends))

    pre = [
        remote(up_ref.at[oc], up_buf.at[up_rows(dp, UPR)], pre_send.at[0], pre_recv.at[0], sibling),
        remote(
            down_ref.at[oc], down_buf.at[down_rows(dp, DNR)],
            pre_send.at[1], pre_recv.at[1], sibling,
        ),
        remote(meta_ref.at[oc], mbuf.at[mine], pre_send.at[2], pre_recv.at[2], sibling),
    ]
    for q in range(Q):
        pre.append(remote(
            grad_ref.at[:, half_cols(oc, q)], gbuf.at[q, tok_rows(mine)],
            pre_send.at[3 + q], pre_recv.at[3 + q], sibling,
        ))
    arrivals = [
        up_buf.at[up_rows(dp_of(xl, z, oc), UPR)],
        down_buf.at[down_rows(dp_of(xl, z, oc), DNR)],
        mbuf.at[theirs],
    ]
    for q in range(Q):
        arrivals.append(gbuf.at[q, tok_rows(theirs)])

    def pre_wait(at):
        remote(arrivals[at], arrivals[at], pre_send.at[at], pre_recv.at[at], sibling).wait_recv()

    def origin(d, s):
        return mod(z - s, NZ) if d == 0 else mod(z + s, NZ)

    def weight_rows(at, xl_, zs):
        dp_ = dp_of(xl_, zs, 0)
        if at == 0:
            return up_buf.at[up_rows(dp_, 2 * UPR)]
        return down_buf.at[down_rows(dp_, 2 * DNR)]

    def ring_parts(kind, d, s, half):
        zs = origin(d, s)
        if kind == "weights":
            return [
                (weight_rows(at, xl, zs), w_send.at[at], w_recv.at[d, at])
                for at in ((d,) if half else (0, 1))
            ]
        block, count = (zs * 2 + d, 1) if half else (zs * 2, 2)
        if kind == "meta":
            return [(mbuf.at[pl.ds(block, count)], m_send, m_recv.at[d])]
        rows = pl.ds(pl.multiple_of(block * TOK, TOK), count * TOK)
        return [(gbuf.at[kind, rows], t_send.at[kind], t_recv.at[d, kind])]

    def ring_send(kind, d, s):
        for block, send, recv in ring_parts(kind, d, s, s == FAR_Z - 1):
            remote(block, block, send, recv.at[s], ring[d]).start()

    def cross(block, at, recv):
        remote(block, block, x_send.at[at], recv, across).start()

    def ring_step(kind, s):
        for d in range(2):
            for block, send, recv in ring_parts(kind, d, s, s == FAR_Z):
                remote(block, block, send, recv.at[s - 1], ring[d]).wait_recv()
            if s < FAR_Z:
                ring_send(kind, d, s)
            if kind == "weights" and s != FAR_Z - 1:
                for at in (d,) if s == FAR_Z else (0, 1):
                    recv = x2_recv.at[at, d] if s == FAR_Z - 2 else x_recv.at[at]
                    cross(weight_rows(at, xl, origin(d, s)), at, recv)

    def wide_copy(d, at, s):
        block = weight_rows(at, oxl, origin(d, s))
        return remote(block, block, e_send.at[d, at], e_recv.at[d, at], ring[d])

    def wide_send(d):
        for at in range(2):
            block = weight_rows(at, oxl, origin(d, FAR_Z - 2))
            remote(block, block, x_send.at[at], x2_recv.at[at, d], across).wait_recv()
            wide_copy(d, at, FAR_Z - 2).start()

    def piece(q):
        pre_wait(3 + q)
        for d in range(2):
            ring_send(q, d, 0)

    def steps(*pairs):
        for kind, at in pairs:
            ring_step(kind, at)

    def far_copy(at):
        src, dst = ((input_ref, far_x), (meta_ref.at[2], far_meta), (grad_ref, far_g))[at]
        return remote(src, dst, f_send.at[at], f_recv.at[at], far)

    def set_out(at, block):
        for d in range(2):
            remote(block, block, w_send.at[at], w_recv.at[d, at, 0], ring[d]).start()
        cross(block, at, x_recv.at[at])

    for copy in pre[:4]:
        copy.start()
    for at in range(3):
        far_copy(at).start()
    set_out(0, up_buf.at[up_rows(dp, UPR)])
    set_out(1, down_buf.at[down_rows(dp, DNR)])
    dispatch_sends(0, 0)
    pre_wait(0)
    set_out(0, arrivals[0])
    pre_wait(1)
    set_out(1, arrivals[1])
    pre_wait(2)
    for d in range(2):
        ring_send("meta", d, 0)
    for copy in pre[4:]:
        copy.start()

    targets = (lax.broadcasted_iota(jnp.int32, (TROWS, TOK), 0) + z * TROWS).astype(F32)

    def select(block):
        cols = pl.ds(pl.multiple_of(block * TOK, TOK), TOK)
        meta = mbuf[block]
        one = jnp.where(targets == meta[1:2, :], meta[3:4, :], 0.0)
        sel[:, cols] = jnp.where(targets == meta[0:1, :], meta[2:3, :], one).astype(BF16)

    def all_bytes(ref, sem):
        pltpu.make_async_copy(ref, ref, sem).wait()

    def others(group):
        return pl.ds(group * SET, (PEERS - 1) * CAP)

    def expert_pre(group):
        all_bytes(got_x.at[others(group)], d_recv.at[group, 0])
        rows = pl.ds(group * SET, SET)

        @pl.loop(0, 2)
        def _(n):
            cols = pl.ds(pl.multiple_of(n * 256, 256), 256)
            pre_buf[:, cols] = jnp.dot(
                got_x[rows, :], up_buf[:, cols], preferred_element_type=F32
            )

    def expert_in(group):
        all_bytes(got_g.at[others(group)], d_recv.at[group, 1])
        rows = pl.ds(group * SET, SET)

        @pl.loop(0, 2)
        def _(n):
            cols = pl.ds(pl.multiple_of(n * 256, 256), 256)
            before = pre_buf[:, cols]
            back = nt_dot(got_g[rows, :], down_buf[cols, :])
            sig = 1.0 / (1.0 + jnp.exp(-before))
            slope_buf[group, :, cols] = (back * sig * (1.0 + before * (1.0 - sig))).astype(BF16)

    def expert_out(group, part):
        rows = pl.ds(group * SET, SET)

        @pl.loop(part * 5, part * 5 + 5)
        def _(n):
            cols = pl.ds(pl.multiple_of(n * 256, 256), 256)
            ret_send[rows, cols] = nt_dot(slope_buf[group], up_buf[cols, :]).astype(BF16)

    def expert_send(group, part):
        cols = slice(part * HALF, (part + 1) * HALF)
        for dy, dc in near:
            y_, c_ = near_at(dy, dc)
            remote(
                ret_send.at[slot_rows(group, y_ * 2 + c_), cols],
                ret_got.at[slot_rows(group, me8), cols],
                r_send.at[group, part], r_recv.at[group, part], dev(x, y_, z, c_),
            ).start()
        ret_got[slot_rows(group, me8), cols] = ret_send[slot_rows(group, me8), cols]

    def returned(group, part):
        cols = pl.ds(part * HALF, HALF)
        all_bytes(ret_got.at[others(group), cols], r_recv.at[group, part])

    def mix_of(blend_ref):
        return blend_ref[pl.ds(pl.multiple_of(xh * SET, SET), SET), :].T.astype(BF16)

    def back_copy(part):
        cols = pl.ds(part * HALF, HALF)
        return remote(
            far_out.at[:, cols], far_back.at[:, cols], b_send.at[part], b_recv.at[part], far
        )

    def far_combine(part):
        returned(1, part)
        mix = mix_of(far_blend)

        @pl.loop(part * 5, part * 5 + 5)
        def _(n):
            cols = pl.ds(pl.multiple_of(n * 256, 256), 256)
            far_out[:, cols] = jnp.dot(
                mix, ret_got[SET : 2 * SET, cols], preferred_element_type=F32
            ).astype(BF16)

        back_copy(part).start()

    def x_rows(x_):
        return pl.ds(pl.multiple_of(x_ * XROWS, XROWS), XROWS)

    def m_rows(m):
        return pl.ds(pl.multiple_of(m * 32, 32), 32)

    def table_part(q):
        @pl.loop(0, TROWS // 256)
        def _(i):
            rows = pl.ds(pl.multiple_of(i * 256, 256), 256)
            dense[q, rows, :] = jnp.dot(
                sel[rows, :], gbuf[q], preferred_element_type=F32
            ).astype(BF16)

        for dx in (1, 3, 2):
            x_ = lax.rem(x + dx, NX)
            remote(
                dense.at[q, x_rows(x_)], s1_got.at[q, dx - 1],
                s1_send.at[q], s1_recv.at[q], dev(x_, y, z, c),
            ).start()

    def table_mid(q):
        all_bytes(s1_got.at[q], s1_recv.at[q])
        total = dense[q, x_rows(x), :].astype(F32)
        for k in range(NX - 1):
            total += s1_got[q, k].astype(F32)
        s2_send[q] = total.astype(BF16)
        for dy, dc in near:
            y_, c_ = near_at(dy, dc)
            remote(
                s2_send.at[q, m_rows(y_ * 2 + c_)], s2_got.at[q, c * NY + y],
                s2_send_sem.at[q], s2_recv.at[q], dev(x, y_, z, c_),
            ).start()
        s2_got[q, c * NY + y] = s2_send[q, m_rows(me8), :]

    def table_sum(q):
        all_bytes(s2_got.at[q, pl.ds(0, PEERS - 1)], s2_recv.at[q])
        for order in range(2):
            total = s2_got[q, order * NY].astype(F32)
            for k in range(1, NY):
                total += s2_got[q, order * NY + k].astype(F32)
            table_ref[order * 2 : order * 2 + 2, :, q * QW : (q + 1) * QW] = total.reshape(
                2, 16, QW
            )

    def sources(s):
        for d in range(2):
            for core in range(2) if s < FAR_Z else (d,):
                select(origin(d, s) * 2 + core)

    def far_inputs():
        far_copy(0).wait_recv()
        far_copy(1).wait_recv()
        choose(far_meta[...], far_pick, far_blend)
        dispatch(1, 0)
        dispatch_sends(1, 0)

    def far_grads():
        far_copy(2).wait_recv()
        dispatch(1, 1)
        dispatch_sends(1, 1)

    def own_grads():
        dispatch(0, 1)
        dispatch_sends(0, 1)

    def own_sources():
        select(mine)
        select(theirs)

    def weights_here():
        all_bytes(up_buf.at[pl.ds(0, 4 * 2 * UPR)], x_recv.at[0])
        all_bytes(down_buf.at[pl.ds(0, 4 * 2 * DNR)], x_recv.at[1])
        for d in range(2):
            for at in range(2):
                wide_copy(d, at, FAR_Z - 1).wait_recv()

    def combine(part):
        mix = mix_of(blend)
        returned(0, part)
        back_copy(part).wait_recv()

        @pl.loop(part * 5, part * 5 + 5)
        def _(n):
            cols = pl.ds(pl.multiple_of(n * 256, 256), 256)
            total = jnp.dot(mix, ret_got[0:SET, cols], preferred_element_type=F32)
            gi_ref[:, cols] = (total + far_back[:, cols].astype(F32)).astype(BF16)

    piece(0)
    own_grads()
    steps(("weights", 1), ("meta", 1))
    ring_step(0, 1)
    own_sources()
    sources(1)
    far_inputs()
    steps(("weights", 2), ("meta", 2))
    ring_step(0, 2)
    piece(1)
    piece(2)
    sources(2)
    far_grads()
    steps(("weights", 3), ("meta", 3))
    ring_step(0, 3)
    sources(3)
    steps(("weights", 4), ("meta", 4))
    wide_send(0)
    wide_send(1)
    sources(4)
    ring_step(0, 4)
    table_part(0)
    ring_step(1, 1)
    ring_step(2, 1)
    weights_here()
    expert_pre(0)
    expert_in(0)
    expert_pre(1)
    ring_step(1, 2)
    ring_step(2, 2)
    expert_out(0, 0)
    expert_send(0, 0)
    ring_step(1, 3)
    ring_step(2, 3)
    piece(3)
    piece(4)
    expert_in(1)
    expert_out(1, 0)
    expert_send(1, 0)
    ring_step(1, 4)
    expert_out(1, 1)
    expert_send(1, 1)
    expert_out(0, 1)
    expert_send(0, 1)
    ring_step(2, 4)
    ring_step(3, 1)
    ring_step(4, 1)
    table_part(1)
    table_mid(0)
    table_part(2)
    ring_step(3, 2)
    ring_step(4, 2)
    table_mid(1)
    ring_step(3, 3)
    ring_step(4, 3)
    far_combine(0)
    table_mid(2)
    ring_step(3, 4)
    table_part(3)
    ring_step(4, 4)
    table_part(4)
    far_combine(1)
    table_sum(0)
    table_sum(1)
    table_sum(2)
    table_mid(3)
    combine(0)
    table_mid(4)
    combine(1)
    table_sum(3)
    table_sum(4)

    for copy in pre:
        copy.wait_send()
    sends = 2 * (NZ - 1)
    all_bytes(up_buf.at[pl.ds(0, (NZ - 1) * 2 * UPR)], w_send.at[0])
    all_bytes(down_buf.at[pl.ds(0, (NZ - 1) * 2 * DNR)], w_send.at[1])
    all_bytes(up_buf.at[pl.ds(0, 6 * 2 * UPR)], x_send.at[0])
    all_bytes(down_buf.at[pl.ds(0, 6 * 2 * DNR)], x_send.at[1])
    for d in range(2):
        for at in range(2):
            wide_copy(d, at, FAR_Z - 2).wait_send()
    all_bytes(mbuf.at[pl.ds(0, sends)], m_send)
    for q in range(Q):
        all_bytes(gbuf.at[q, pl.ds(0, sends * TOK)], t_send.at[q])
        all_bytes(s1_got.at[q], s1_send.at[q])
        all_bytes(s2_got.at[q, pl.ds(0, PEERS - 1)], s2_send_sem.at[q])
    for at in range(3):
        far_copy(at).wait_send()
    for group in range(2):
        all_bytes(send_x.at[others(group)], d_send.at[group, 0])
        all_bytes(send_g.at[others(group)], d_send.at[group, 1])
        for part in range(2):
            all_bytes(ret_send.at[others(group), pl.ds(part * HALF, HALF)], r_send.at[group, part])
    for part in range(2):
        back_copy(part).wait_send()


def per_device(
    grad_out, saved_input, expert_ids, gate_weights, up_weight, down_weight,
    engram_gate, memory_owner, memory_slot,
):
    head = jnp.arange(4, dtype=jnp.int32)[None, :] % 2
    core = memory_owner % 2
    zs = (memory_owner // 2) % NZ
    xs = memory_owner // (2 * NZ)
    to = memory_slot // 16
    xs = (to // NY) * 2 + xs
    row = (((zs * NX + xs) * NY + to % NY) * 2 + core) * 32
    row = row + head * 16 + memory_slot % 16
    rows = jnp.concatenate([row, expert_ids], axis=1).astype(F32)
    gates = jnp.concatenate([engram_gate, gate_weights], axis=1)
    meta = jnp.concatenate(
        [
            rows.T.reshape(3, 2, TOK),
            gates.T.reshape(3, 2, TOK),
            jnp.zeros((3, 4, TOK), F32),
        ],
        axis=1,
    )

    vmem = pl.BlockSpec(memory_space=pltpu.VMEM)
    dma = pltpu.SemaphoreType.DMA
    return pl.pallas_call(
        kernel,
        out_shape=(
            jax.ShapeDtypeStruct((TOK, D), BF16),
            jax.ShapeDtypeStruct((4, 16, HALF), F32),
        ),
        in_specs=[vmem] * 5,
        out_specs=(vmem, vmem),
        scratch_shapes=[
            pltpu.VMEM((D, HID), BF16),
            pltpu.VMEM((HID, D), BF16),
            pltpu.VMEM((TOK, D), BF16),
            pltpu.VMEM((TOK, D), BF16),
            pltpu.VMEM((8, TOK), F32),
            pltpu.VMEM((EXPERTS * CAP, TOK), BF16),
            pltpu.VMEM((EXPERTS * CAP, TOK), BF16),
            pltpu.VMEM((EXPERTS * CAP, TOK), F32),
            pltpu.VMEM((EXPERTS * CAP, TOK), F32),
            pltpu.VMEM((EXPERTS * CAP, D), BF16),
            pltpu.VMEM((EXPERTS * CAP, D), BF16),
            pltpu.VMEM((EXPERTS * CAP, D), BF16),
            pltpu.VMEM((EXPERTS * CAP, D), BF16),
            pltpu.VMEM((SET, HID), F32),
            pltpu.VMEM((2, SET, HID), BF16),
            pltpu.VMEM((EXPERTS * CAP, D), BF16),
            pltpu.VMEM((EXPERTS * CAP, D), BF16),
            pltpu.VMEM((TOK, D), BF16),
            pltpu.VMEM((TOK, D), BF16),
            pltpu.VMEM((Q, BLOCKS * TOK, QW), BF16),
            pltpu.VMEM((BLOCKS, 8, TOK), F32),
            pltpu.VMEM((TROWS, BLOCKS * TOK), BF16),
            pltpu.VMEM((Q, TROWS, QW), BF16),
            pltpu.VMEM((Q, NX - 1, XROWS, QW), BF16),
            pltpu.VMEM((Q, XROWS, QW), BF16),
            pltpu.VMEM((Q, PEERS, 32, QW), BF16),
            dma((3 + Q,)),
            dma((3 + Q,)),
            dma((2, 2, FAR_Z)),
            dma((2,)),
            dma((2,)),
            dma((2, 2)),
            dma((2,)),
            dma((2, 2)),
            dma((2, 2)),
            dma((2, FAR_Z)),
            dma(()),
            dma((2, Q, FAR_Z)),
            dma((Q,)),
            dma((3,)),
            dma((3,)),
            dma((2, 2)),
            dma((2, 2)),
            dma((2, 2)),
            dma((2, 2)),
            dma((2,)),
            dma((2,)),
            dma((Q,)),
            dma((Q,)),
            dma((Q,)),
            dma((Q,)),
        ],
        compiler_params=pltpu.CompilerParams(
            collective_id=0, has_side_effects=True, vmem_limit_bytes=58 * 1024 * 1024
        ),
        cost_estimate=pl.CostEstimate(
            flops=10_000_000_000, bytes_accessed=4_000_000, transcendentals=262_144
        ),
    )(grad_out, saved_input, up_weight, down_weight, meta)


def solution(mesh):
    tokens = P(("dp", "expert"), None)
    return jax.shard_map(
        per_device,
        mesh=mesh,
        in_specs=(
            tokens, tokens, tokens, tokens,
            P("expert", "dp", None), P("expert", "dp", None),
            tokens, tokens, tokens,
        ),
        out_specs=(tokens, P(None, ("dp", "expert"), None)),
        check_vma=False,
    )
```
